256 devices in a mesh: ens: 8 (over z_lo, y), space: 32 (over x, z_hi, core).
Axes of the slice: x: 4, y: 4, z: 8 (z_hi: 4, z_lo: 2; z = z_hi * 2 + z_lo), core: 2. Of those that a mesh axis runs over, the one named last changes fastest.
Arguments:
- hidden: bfloat16 [8, 1024, 32768], P('ens', None, 'space'), may hold values from -6 to 6
- target: float32 [100, 32768], P(None, 'space'), may hold values from -6 to 6
- area_index: int32 [32768], P('space'), may hold values from 0 to 720
- area_table: float32 [721], replicated, may hold values from 0.1 to 3
- var_weight: float32 [100], replicated, may hold values from 0.25 to 2
- w_first: bfloat16 [1024, 1024], replicated, may hold values from -0.1875 to 0.1875
- b_first: float32 [1024], replicated, may hold values from -3 to 3
- w_second: bfloat16 [1024, 100], replicated, may hold values from -0.1875 to 0.1875
- b_second: float32 [100], replicated, may hold values from -3 to 3
Outputs:
- loss: float32 [], replicated
- grad_hidden: bfloat16 [8, 1024, 32768], P('ens', None, 'space')
- grad_w_first: float32 [1024, 1024], P('space')
- grad_b_first: float32 [1024], P('space')
- grad_w_second: float32 [1024, 100], P('space')
- grad_b_second: float32 [100], replicated
The draws below stay inside these ranges and needn't reach their ends.
All inputs are finite; a program needn't handle non-finite values.
Results may differ from the reference program's by a relative error of at most 0.011.
Values sent between devices are 32-bit elements; how exact they have to be, the bound alone decides.
No kernel may reach another device: no remote copies, remote signals or barrier semaphores. Data moves between devices by JAX's collectives and lax.ppermute only.
A program may use at most 64 MiB of HBM per device.

```python
import math
import jax
import jax.numpy as jnp
from jax import lax

C = 1024
V = 100
NLAT = 721
MEMBERS = 8
POINTS = 32768


def draw_area_index(key, part):
    key = jax.random.fold_in(key, 11)
    base = jnp.arange(POINTS, dtype=jnp.int32) * NLAT // POINTS
    jitter = jax.random.randint(key, (POINTS,), -2, 3, dtype=jnp.int32)
    rows = jnp.clip(base + jitter, 0, NLAT - 1)
    rows = rows.at[0].set(0)
    return rows.at[POINTS - 1].set(NLAT - 1).astype(jnp.int32)


def draw_area_table(key, part):
    key = jax.random.fold_in(key, 23)
    level = jnp.arange(NLAT, dtype=jnp.float32) / (NLAT - 1)
    factor = jax.random.uniform(key, (NLAT,), jnp.float32, 0.7, 1.4)
    base = 0.25 + level
    return (base * factor).astype(jnp.float32)


def spiked(result, stream_key, source, target, parts, factor):
    def block_of(dim):
        return (jnp.arange(result.shape[dim]) // (result.shape[dim] // parts)).reshape((-1,) + (1,) * (result.ndim - 1 - dim))

    one_side = jax.random.permutation(stream_key, parts)[block_of(target)]
    far = (block_of(target) + parts // 2) % parts
    return jnp.where((block_of(source) == one_side) | (block_of(source) == far), factor * result, result)


def shard_levels(own_key, dims, shards, low, largest):
    level, own = 1.0, jax.random.fold_in(own_key, 6)
    for position, blocks in shards:
        heights = jnp.exp(jax.random.uniform(jax.random.fold_in(own, position), (blocks,), jnp.float32, low / len(shards), largest / len(shards)))
        level = level * jnp.repeat(heights, dims[position] // blocks).reshape([-1 if axis == position else 1 for axis in range(len(dims))])
    return level


def gaussian(rng, extent, scale, reach, cuts=(), kind=jnp.bfloat16):
    factor_of = shard_levels(rng, extent, cuts, -0.22, 0.18) if cuts else 1.0
    array = jax.random.normal(rng, extent, jnp.float32) * scale * factor_of
    return jnp.minimum(jnp.maximum(array, -reach), reach).astype(kind)


def gaussian_with(key, dims, scale, limit, split, heavy, kind=jnp.bfloat16):
    array = scale * jax.random.normal(key, dims, jnp.float32)
    if split:
        array = array * shard_levels(key, dims, split, -0.22, 0.18)
    return jnp.clip(spiked(array, jax.random.fold_in(key, 3), *heavy), -limit, limit).astype(kind)


def setup_inputs(seed: int = 0) -> dict:
    arg_keys = jax.random.split(jax.random.key(seed), 10)
    return {
        "hidden": gaussian_with(arg_keys[0], (MEMBERS, C, POINTS), 1.0, 6.0, ((0, 8), (2, 32)), (2, 1, 32, 2.75)),
        "target": gaussian(arg_keys[1], (V, POINTS), 1.0, 6.0, ((1, 32),), jnp.float32),
        "area_index": draw_area_index(jax.random.fold_in(arg_keys[9], 71), 0),
        "area_table": draw_area_table(jax.random.fold_in(arg_keys[9], 71), 0),
        "var_weight": jnp.clip(jnp.exp(jax.random.uniform(arg_keys[4], (V,), jnp.float32, math.log(0.25), math.log(2.0))), 0.25, 2.0),
        "w_first": gaussian(arg_keys[5], (C, C), C ** -0.5, 0.1875),
        "b_first": gaussian(arg_keys[6], (C,), 0.5, 3.0, (), jnp.float32),
        "w_second": gaussian(arg_keys[7], (C, V), C ** -0.5, 0.1875),
        "b_second": gaussian(arg_keys[8], (V,), 0.5, 3.0, (), jnp.float32),
    }


smoothing = 0.0025
loss_scale = 64.0

def reference(hidden, target, area_index, area_table, var_weight, w_first, b_first, w_second, b_second):
    coef = var_weight[:, None] * area_table[area_index][None, :]
    fields = []
    for member in range(MEMBERS):
        pre = jnp.dot(w_first.T, hidden[member], preferred_element_type=jnp.float32) + b_first[:, None]
        hidden_act = jax.nn.gelu(pre).astype(jnp.bfloat16)
        fields.append(jnp.dot(w_second.T, hidden_act, preferred_element_type=jnp.float32) + b_second[:, None])
    stacked = jnp.stack(fields)
    total = jnp.float32(0.0)
    grad_w1 = jnp.zeros((C, C), jnp.float32)
    grad_w2 = jnp.zeros((C, V), jnp.float32)
    grad_b1 = jnp.zeros((C,), jnp.float32)
    grad_b2 = jnp.zeros((V,), jnp.float32)
    grads_hidden = []
    for member in range(MEMBERS):
        mine = stacked[member]
        differ = mine[None] - stacked
        radius = jnp.sqrt(differ * differ + smoothing)
        spread = lax.optimization_barrier(jnp.sum(radius, axis=0))
        pull = lax.optimization_barrier(jnp.sum(differ / radius, axis=0))
        miss = mine - target
        skill = jnp.sqrt(miss * miss + smoothing)
        crps = skill / MEMBERS - spread / (2.0 * MEMBERS * (MEMBERS - 1))
        total = total + jnp.sum(coef * crps)
        slope = miss / skill / MEMBERS - pull / (1.0 * MEMBERS * (MEMBERS - 1))
        grad_x = (loss_scale * coef * slope).astype(jnp.bfloat16)
        pre = jnp.dot(w_first.T, hidden[member], preferred_element_type=jnp.float32) + b_first[:, None]
        hidden_act = jax.nn.gelu(pre).astype(jnp.bfloat16)
        grad_z = jnp.dot(w_second, grad_x, preferred_element_type=jnp.float32)
        grad_pre = jax.vjp(jax.nn.gelu, pre)[1](grad_z)[0].astype(jnp.bfloat16)
        grads_hidden.append(jnp.dot(w_first, grad_pre, preferred_element_type=jnp.float32).astype(jnp.bfloat16))
        grad_w1 = grad_w1 + jnp.dot(hidden[member], grad_pre.T, preferred_element_type=jnp.float32)
        grad_w2 = grad_w2 + jnp.dot(hidden_act, grad_x.T, preferred_element_type=jnp.float32)
        grad_b1 = grad_b1 + lax.optimization_barrier(jnp.sum(grad_pre.astype(jnp.float32), axis=1))
        grad_b2 = grad_b2 + lax.optimization_barrier(jnp.sum(grad_x.astype(jnp.float32), axis=1))
    factor = 1.0 / math.sqrt(MEMBERS * POINTS)
    loss = total / POINTS
    return (loss, jnp.stack(grads_hidden), grad_w1 * factor, grad_b1 * factor, grad_w2 * factor, grad_b2 * factor)
```

```python
import math

import jax
import jax.numpy as jnp
from jax import lax
from jax.sharding import Mesh, PartitionSpec as P

smoothing = 0.0025
loss_scale = 64.0
ens = ("zl", "y")
space = ("x", "zh", "c")
plane = ("y", "x")
wide = 1152


def on_device(
    hidden, target, area_index, area_table, var_weight, w_first, b_first, w_second, b_second
):
    f32, bf16 = jnp.float32, jnp.bfloat16
    members = lax.axis_size(ens)
    columns = hidden.shape[2]
    variables = target.shape[0]
    channels = w_first.shape[0]
    slab = columns // members
    me = lax.axis_index(ens)
    features = hidden[0]
    pre = jnp.einsum("io,ip->op", w_first, features, preferred_element_type=f32) + b_first[:, None]
    hidden_act = jax.nn.gelu(pre).astype(bf16)
    mine = (
        jnp.einsum("ov,op->vp", w_second, hidden_act, preferred_element_type=f32)
        + b_second[:, None]
    )
    pieces = mine.reshape(variables, members, slab).transpose(1, 0, 2)
    fields = lax.all_to_all(pieces, ens, 0, 0)
    rows = lax.dynamic_slice_in_dim(area_index, me * slab, slab, 0)
    goal = lax.dynamic_slice_in_dim(target, me * slab, slab, 1)
    table_rows = area_table.shape[0]
    onehot = (rows[:, None] == jnp.arange(table_rows, dtype=jnp.int32)[None, :]).astype(f32)
    area = jnp.dot(onehot, area_table, precision=lax.Precision.HIGHEST)
    coef = var_weight[:, None] * area[None, :]
    differ = fields[:, None] - fields[None, :]
    radius = jnp.sqrt(differ * differ + smoothing)
    spread = jnp.sum(radius, axis=1)
    pull = jnp.sum(differ / radius, axis=1)
    miss = fields - goal[None]
    skill = jnp.sqrt(miss * miss + smoothing)
    crps = skill / members - spread / (2.0 * members * (members - 1))
    loss_part = jnp.sum(coef[None] * crps)
    slope = miss / skill / members - pull / (1.0 * members * (members - 1))
    slope = coef[None] * slope
    part_b2 = jnp.sum((loss_scale * slope).astype(bf16).astype(f32), axis=(0, 2))
    back = loss_scale * lax.all_to_all(slope, ens, 0, 0)
    grad_x = back.transpose(1, 0, 2).reshape(variables, columns).astype(bf16)
    grad_z = jnp.einsum("ov,vp->op", w_second, grad_x, preferred_element_type=f32)
    grad_pre = jax.vjp(jax.nn.gelu, pre)[1](grad_z)[0].astype(bf16)
    part_w1 = jnp.einsum("ip,op->io", features, grad_pre, preferred_element_type=f32)
    part_w2 = jnp.einsum("op,vp->ov", hidden_act, grad_x, preferred_element_type=f32)
    part_b1 = jnp.sum(grad_pre.astype(f32), axis=1)
    nx, nzh, nc, ny = (lax.axis_size(a) for a in ("x", "zh", "c", "y"))
    share = channels // (nx * nzh * nc)
    misc = jnp.concatenate([part_b2, loss_part[None], jnp.zeros((27,), f32)]).reshape(4, share).T
    misc = jnp.tile(misc, (channels // share, 1))
    spare = wide - channels - variables - 1 - 4
    part = jnp.concatenate(
        [part_w1, part_w2, part_b1[:, None], misc, jnp.zeros((channels, spare), f32)], axis=1
    )
    part = part.reshape(nx, nzh, nc, ny, share // ny, wide)
    core = lax.axis_index("c")
    keep = lax.dynamic_index_in_dim(part, core, 2, keepdims=False)
    send = lax.dynamic_index_in_dim(part, 1 - core, 2, keepdims=False)
    other = lax.ppermute(send, "c", [(0, 1), (1, 0)])
    grad_feat = jnp.einsum("io,op->ip", w_first, grad_pre, preferred_element_type=f32).astype(bf16)
    half = (keep + other).transpose(2, 0, 1, 3, 4).reshape(ny * nx, nzh, share // ny, wide)
    half = jnp.sum(lax.all_to_all(half, plane, 0, 0), axis=0)
    half = jnp.sum(lax.all_to_all(half, "zh", 0, 0), axis=0)
    whole = lax.all_to_all(jnp.broadcast_to(half[None], (members,) + half.shape), ens, 0, 0)
    whole = whole.reshape(members // ny, ny, share // ny, wide).sum(0).reshape(share, wide)
    total_points = columns * lax.axis_size(space)
    factor = 1.0 / math.sqrt(members * total_points)
    sums = whole[:, channels + variables + 1 : channels + variables + 5].T.reshape(-1)
    return (
        sums[variables] / total_points,
        grad_feat[None],
        whole[:, :channels] * factor,
        whole[:, channels + variables] * factor,
        whole[:, channels : channels + variables] * factor,
        sums[:variables] * factor,
    )


def solution(mesh):
    fine = Mesh(mesh.devices.reshape(2, 4, 4, 4, 2), ("zl", "y", "x", "zh", "c"))
    in_specs = (P(ens, None, space), P(None, space), P(space), P(), P(), P(), P(), P(), P())
    out_specs = (P(), P(ens, None, space), P(space, None), P(space), P(space, None), P())
    return jax.shard_map(
        on_device, mesh=fine, in_specs=in_specs, out_specs=out_specs, check_vma=False
    )
```

```python
import functools
import math

import jax
import jax.numpy as jnp
from jax import lax
from jax.experimental import pallas as pl
from jax.experimental.pallas import tpu as pltpu
from jax.sharding import Mesh, PartitionSpec as P

smoothing = 0.0025
loss_scale = 64.0
ens = ("zl", "y")
space = ("x", "zh", "c")
plane = ("y", "x", "c")
lanes = 128
tile = 256
f32, bf16 = jnp.float32, jnp.bfloat16
root = math.sqrt(2.0 / math.pi)
cubic = 0.044715


def dot(a, b, contract):
    return lax.dot_general(a, b, (contract, ((), ())), preferred_element_type=f32)


hbm = pl.BlockSpec(memory_space=pltpu.HBM)
near = pl.BlockSpec(memory_space=pltpu.VMEM)


def call(kernel, out_shape, ins, outs, scratch=(), flops=0, limit=24):
    return pl.pallas_call(
        kernel,
        out_shape=out_shape,
        in_specs=ins,
        out_specs=outs,
        scratch_shapes=scratch,
        compiler_params=pltpu.CompilerParams(vmem_limit_bytes=limit * 2**20),
        cost_estimate=pl.CostEstimate(flops=flops, bytes_accessed=2**22, transcendentals=0),
    )


def columns_of(row, width):
    return jnp.transpose(jnp.broadcast_to(row, (width, row.shape[1])))


def arrive(pairs, sems):
    copies = [pltpu.make_async_copy(s, d, sems.at[i]) for i, (s, d) in enumerate(pairs)]
    for c in copies:
        c.start()
    return copies


def turn(w, wt):
    for j in range(0, w.shape[1], tile):
        wt[j : j + tile, :] = jnp.transpose(w[:, j : j + tile])


def forward_kernel(
    f_hbm, w_hbm, b1_hbm, w2_hbm, b2_hbm, x_ref, wt_hbm, f, w, b1, w2, b2, wt, sems, outs
):
    channels = w.shape[1]
    parts = [pl.ds(j, tile) for j in range(0, channels, tile)]
    copies = arrive(
        [(w_hbm.at[:, p], w.at[:, p]) for p in parts]
        + [(f_hbm, f), (b1_hbm, b1), (w2_hbm, w2), (b2_hbm, b2)],
        sems,
    )
    sent = []
    for j, p in enumerate(parts):
        copies[j].wait()
        wt[p, :] = jnp.transpose(w[:, p])
        c = pltpu.make_async_copy(wt.at[p, :], wt_hbm.at[p, :], outs.at[j])
        c.start()
        sent.append(c)
    for c in copies[len(parts) :]:
        c.wait()
    shift = columns_of(b1[...], lanes)
    bias = columns_of(b2[...], lanes)
    pre = dot(wt[...], f[...], ((1,), (0,))) + jnp.tile(shift, (1, f.shape[1] // lanes))
    t = jnp.tanh(pre * (root + (root * cubic) * (pre * pre)))
    z = (0.5 * pre * (1.0 + t)).astype(bf16)
    x = dot(w2[...], z, ((1,), (0,)))
    for m in range(x_ref.shape[0]):
        x_ref[m] = x[:, m * lanes : (m + 1) * lanes] + bias
    for c in sent:
        c.wait()


def again_kernel(x_hbm, f_hbm, wt_hbm, b1_hbm, z_hbm, g_hbm, f, wt, b1, z, g, sems, outs):
    points = f.shape[1]
    parts = [pl.ds(q, tile) for q in range(0, points, tile)]
    copies = arrive(
        [(b1_hbm, b1), (wt_hbm, wt)] + [(f_hbm.at[:, p], f.at[:, p]) for p in parts], sems
    )
    copies[0].wait()
    shift = jnp.tile(columns_of(b1[...], lanes), (1, tile // lanes))
    copies[1].wait()
    sent = []
    for k, here in enumerate(parts):
        copies[2 + k].wait()
        pre = dot(wt[...], f[:, here], ((1,), (0,))) + shift
        square = pre * pre
        t = jnp.tanh(pre * (root + (root * cubic) * square))
        z[:, here] = (0.5 * pre * (1.0 + t)).astype(bf16)
        inner = root + (3.0 * root * cubic) * square
        g[:, here] = (0.5 * ((1.0 + t) + (pre * inner) * (1.0 - t * t))).astype(bf16)
        for i, (s, d) in enumerate(((z, z_hbm), (g, g_hbm))):
            c = pltpu.make_async_copy(s.at[:, here], d.at[:, here], outs.at[k, i])
            c.start()
            sent.append(c)
    for c in sent:
        c.wait()


def pair_kernel(
    z_hbm, x_ref, goal_hbm, index_hbm, table_hbm, weight_hbm, dx_ref, misc_ref,
    col, goal_ref, index_ref, table_ref, weight_ref, sems,
):
    members, variables, slab = x_ref.shape
    me = lax.axis_index(ens)
    here = pl.ds(pl.multiple_of(me * slab, slab), slab)
    rows = table_ref.shape[1]
    copies = arrive(
        [
            (index_hbm, index_ref),
            (table_hbm, table_ref),
            (weight_hbm, weight_ref),
            (goal_hbm.at[:, here], goal_ref),
        ],
        sems,
    )
    fields = [x_ref[m] for m in range(members)]
    pull = [None] * members
    spread = None
    for a in range(members):
        for b in range(a + 1, members):
            d = fields[a] - fields[b]
            square = d * d + smoothing
            inverse = lax.rsqrt(square)
            spread = square * inverse if spread is None else spread + square * inverse
            term = d * inverse
            pull[a] = term if pull[a] is None else pull[a] + term
            pull[b] = -term if pull[b] is None else pull[b] - term
    spread = 2.0 * spread + members * math.sqrt(smoothing)
    for c in copies:
        c.wait()
    hot = lax.broadcasted_iota(jnp.int32, (rows, slab), 0) == index_ref[:, here]
    area = lax.dot_general(
        table_ref[...],
        hot.astype(f32),
        (((1,), (0,)), ((), ())),
        precision=lax.Precision.HIGHEST,
        preferred_element_type=f32,
    )
    coef = columns_of(weight_ref[...], slab) * area
    goal = goal_ref[...]
    pairs = members * (members - 1)
    skills = None
    total = None
    for m in range(members):
        miss = fields[m] - goal
        square = miss * miss + smoothing
        inverse = lax.rsqrt(square)
        skills = square * inverse if skills is None else skills + square * inverse
        slope = miss * inverse * (1.0 / members) - pull[m] * (1.0 / pairs)
        grad = (loss_scale * coef * slope).astype(bf16).astype(f32)
        dx_ref[m] = grad
        total = grad if total is None else total + grad
    crps = coef * (skills * (1.0 / members) - spread * (0.5 / pairs))
    col[...] = jnp.zeros_like(col)
    col[:variables, :] = jnp.broadcast_to(jnp.sum(total, axis=1, keepdims=True), (variables, lanes))
    loss = jnp.sum(jnp.sum(crps, axis=0, keepdims=True), axis=1, keepdims=True)
    col[variables : variables + 1, :] = jnp.broadcast_to(loss, (1, lanes))
    share = misc_ref.shape[0]
    lane = lax.broadcasted_iota(jnp.int32, (share, lanes), 1)
    out = jnp.zeros((share, lanes), f32)
    for g in range(lanes // share):
        out = jnp.where(lane == variables + 1 + g, col[g * share : (g + 1) * share, :], out)
    misc_ref[...] = out


def scatter_rows(first, put, nx, nzh, ny, rows):
    for y in range(ny):
        for zh in range(nzh):
            for x in range(nx):
                r = ((x * nzh + zh) * ny + y) * rows
                put(y, x, zh, first[r : r + rows])


def send_kernel(
    back_ref, w2_ref, misc_ref, g_hbm, z_hbm, f_hbm, dpre_ref, send_ref, keep_ref, dx, g, z, f, piece, sems
):
    members, variables, slab = back_ref.shape
    ny, nx, nzh, rows, _ = send_ref.shape
    channels, points = z.shape
    share = ny * rows
    core = lax.axis_index("c")
    steps = channels // tile
    copies = []
    for j in range(steps):
        here = pl.ds(j * tile, tile)
        copies += [(g_hbm.at[here, :], g.at[here, :]), (z_hbm.at[here, :], z.at[here, :])]
        if j == 0:
            copies.append((f_hbm.at[:, 1 - core], f))
    copies = arrive(copies, sems)
    dx[...] = jnp.zeros_like(dx)
    for m in range(members):
        dx[:variables, m * slab : (m + 1) * slab] = back_ref[m].astype(bf16)
    lane = lax.broadcasted_iota(jnp.int32, (tile, lanes), 1)
    extra = jnp.tile(misc_ref[...], (tile // share, 1))
    half = None
    for j in range(steps):
        here = slice(j * tile, (j + 1) * tile)
        w2j = jnp.transpose(w2_ref[:, here])
        copies[0 if j == 0 else 2 * j + 1].wait()
        dz = dot(w2j, dx[:variables, :], ((1,), (0,)))
        d = (dz * g[here, :].astype(f32)).astype(bf16)
        dpre_ref[here, :] = d
        sums = jnp.sum(d.astype(f32), axis=1, keepdims=True)
        copies[1 if j == 0 else 2 * j + 2].wait()
        second = dot(z[here, :], dx[...], ((1,), (1,)))
        second = jnp.where(lane == variables, sums, second + extra)
        piece[...] = second.reshape(nzh, 2, share, lanes)
        go, stay = piece[:, 1 - core], piece[:, core]
        if j == 0:
            copies[2].wait()
            half = f[...].reshape(f.shape[0] * share, points)
        first = dot(half, d, ((1,), (1,)))
        for y in range(ny):
            for zh in range(nzh):
                send_ref[y, j, zh, :, channels:] = go[zh, y * rows : (y + 1) * rows]
                keep_ref[y, j, zh] = stay[zh, y * rows : (y + 1) * rows]

        def put(y, x, zh, value):
            send_ref[y, x, zh, :, here] = value

        scatter_rows(first, put, nx, nzh, ny, rows)


def window_kernel(d_ref, w_hbm, f_hbm, own_ref, grad_hbm, w, f, grad, sems, outs):
    ny, nx, nzh, rows, channels = own_ref.shape
    points = d_ref.shape[1]
    share = ny * rows
    core = lax.axis_index("c")
    copies = arrive([(f_hbm.at[:, core], f), (w_hbm, w)], sems)
    copies[0].wait()
    half = f[...].reshape(f.shape[0] * share, points)
    first = dot(half, d_ref[...], ((1,), (1,)))

    def put(y, x, zh, value):
        own_ref[y, x, zh] = value

    scatter_rows(first, put, nx, nzh, ny, rows)
    copies[1].wait()
    sent = []
    side = channels // 2
    for k in range(2):
        here = pl.ds(k * side, side)
        grad[here, :] = dot(w[here, :], d_ref[...], ((1,), (0,))).astype(bf16)
        c = pltpu.make_async_copy(grad.at[here, :], grad_hbm.at[here, :], outs.at[k])
        c.start()
        sent.append(c)
    for c in sent:
        c.wait()


def add_kernel(own_ref, keep_ref, other_ref, out_ref):
    ny, nx, nzh, rows, channels = own_ref.shape
    core = lax.axis_index("c")
    for y in range(ny):
        for x in range(nx):
            a = jnp.where(core == 0, y, x)
            b = jnp.where(core == 0, x, y)
            for zh in range(nzh):
                here = pl.ds(zh * rows, rows)
                out_ref[a, b, here, :channels] = (
                    own_ref[y, x, zh] + other_ref[y, x, zh, :, :channels]
                )
                out_ref[a, b, here, channels:] = (
                    keep_ref[y, x, zh] + other_ref[y, x, zh, :, channels:]
                )


def deal_kernel(axes, in_ref, *out_refs):
    core = lax.axis_index("c")
    me = jnp.where(core == 0, lax.axis_index(axes[0]), lax.axis_index(axes[1]))
    n = len(out_refs)
    for d in range(n):
        k = lax.rem(me + d, n)
        total = in_ref[0, k]
        for i in range(1, in_ref.shape[0]):
            total = total + in_ref[i, k]
        out_refs[d][...] = total


def redeal_kernel(axis, *refs):
    n = len(refs) // 2
    me = lax.axis_index(axis)
    rows = refs[n].shape[0]
    for d in range(n):
        here = pl.ds(pl.multiple_of(lax.rem(me + d, n) * rows, rows), rows)
        total = refs[0][here, :]
        for i in range(1, n):
            total = total + refs[i][here, :]
        refs[n + d][...] = total


def spread_kernel(*refs):
    out_ref = refs[-1]
    total = refs[0][...]
    for r in refs[1:-1]:
        total = total + r[...]
    for i in range(out_ref.shape[0]):
        out_ref[i] = total


def finish_kernel(factor, points, in_ref, w1_ref, b1_ref, w2_ref, b2_ref, loss_ref, part):
    ny = in_ref.shape[0] // 2
    rows = in_ref.shape[1]
    share, channels = w1_ref.shape
    variables = w2_ref.shape[1]
    part[...] = jnp.zeros_like(part)
    for y in range(ny):
        here = slice(y * rows, (y + 1) * rows)
        w1_ref[here, :] = (in_ref[y, :, :channels] + in_ref[ny + y, :, :channels]) * factor
        part[here, :] = in_ref[y, :, channels:] + in_ref[ny + y, :, channels:]
    w2_ref[...] = part[:share, :variables] * factor
    turned = jnp.transpose(part[...])
    b1_ref[...] = turned[variables : variables + 1, :share] * factor
    line = turned[variables + 1 : variables + 2, :]
    for g in range(1, lanes // share):
        line = line + pltpu.roll(turned[variables + 1 + g : variables + 2 + g, :], g * share, 1)
    b2_ref[...] = line[:, :variables] * factor
    loss_ref[...] = line[:, variables : variables + 1] * (1.0 / points)


def lines(ny, nx):
    at = lambda y, x, c: (y * nx + x) * 2 + c
    down = [[at(y, x, 0) for y in range(ny)] for x in range(nx)]
    along = [[at(y, x, 1) for x in range(nx)] for y in range(ny)]
    return down + along


def shifts(ny, nx, d):
    at = lambda y, x, c: (y * nx + x) * 2 + c
    pairs = [(at(y, x, 0), at(y, (x + d) % nx, 0)) for y in range(ny) for x in range(nx)]
    return pairs + [(at(y, x, 1), at((y + d) % ny, x, 1)) for y in range(ny) for x in range(nx)]


def on_device(
    hidden, target, area_index, area_table, var_weight, w_first, b_first, w_second, b_second
):
    members = lax.axis_size(ens)
    columns = hidden.shape[2]
    variables = target.shape[0]
    channels = w_first.shape[0]
    slab = columns // members
    nx, nzh, nc, ny = (lax.axis_size(a) for a in ("x", "zh", "c", "y"))
    share = channels // (nx * nzh * nc)
    rows = share // ny
    wide = channels + lanes
    shape = jax.ShapeDtypeStruct
    features = hidden[0]
    grouped = features.reshape(nx * nzh, nc, share, columns)
    w2t = w_second.T
    square = (channels, columns)
    dma = pltpu.SemaphoreType.DMA
    mine, wt = call(
        forward_kernel,
        (shape((members, variables, slab), f32), shape((channels, channels), bf16)),
        [hbm] * 5,
        (near, hbm),
        scratch=[
            pltpu.VMEM(square, bf16),
            pltpu.VMEM((channels, channels), bf16),
            pltpu.VMEM((1, channels), f32),
            pltpu.VMEM((variables, channels), bf16),
            pltpu.VMEM((1, variables), f32),
            pltpu.VMEM((channels, channels), bf16),
            dma((8,)),
            dma((4,)),
        ],
        flops=2 * channels * channels * columns,
        limit=60,
    )(features, w_first, b_first[None], w2t, b_second[None])
    fields = lax.all_to_all(mine, ens, 0, 0)
    z, g = call(
        again_kernel,
        (shape(square, bf16), shape(square, bf16)),
        [pl.BlockSpec(memory_space=pl.ANY)] + [hbm] * 3,
        (hbm, hbm),
        scratch=[
            pltpu.VMEM(square, bf16),
            pltpu.VMEM((channels, channels), bf16),
            pltpu.VMEM((1, channels), f32),
            pltpu.VMEM(square, bf16),
            pltpu.VMEM(square, bf16),
            dma((6,)),
            dma((4, 2)),
        ],
        flops=2 * channels * channels * columns,
        limit=60,
    )(mine, features, wt, b_first[None])
    dx, misc = call(
        pair_kernel,
        (shape((members, variables, slab), f32), shape((share, lanes), f32)),
        [pl.BlockSpec(memory_space=pl.ANY), near] + [hbm] * 4,
        (near, near),
        scratch=[
            pltpu.VMEM((lanes, lanes), f32),
            pltpu.VMEM((variables, slab), f32),
            pltpu.VMEM((1, columns), jnp.int32),
            pltpu.VMEM((1, area_table.shape[0]), f32),
            pltpu.VMEM((1, variables), f32),
            dma((4,)),
        ],
        limit=60,
    )(z, fields, target, area_index[None], area_table[None], var_weight[None])
    back = lax.all_to_all(dx, ens, 0, 0)
    part = (ny, nx, nzh, rows)
    dpre, send, keep = call(
        send_kernel,
        (shape(square, bf16), shape(part + (wide,), f32), shape(part + (lanes,), f32)),
        [near] * 3 + [hbm] * 3,
        (near, near, near),
        scratch=[
            pltpu.VMEM((lanes, columns), bf16),
            pltpu.VMEM(square, bf16),
            pltpu.VMEM(square, bf16),
            pltpu.VMEM((nx * nzh, share, columns), bf16),
            pltpu.VMEM((nzh, nc, share, lanes), f32),
            dma((9,)),
        ],
        flops=channels * channels * columns,
        limit=24,
    )(back, w2t, misc, g, z, grouped)
    other = lax.ppermute(send, "c", [(0, 1), (1, 0)])
    own, grad_feat = call(
        window_kernel,
        (shape(part + (channels,), f32), shape(square, bf16)),
        [near, hbm, hbm],
        (near, hbm),
        scratch=[
            pltpu.VMEM((channels, channels), bf16),
            pltpu.VMEM((nx * nzh, share, columns), bf16),
            pltpu.VMEM(square, bf16),
            dma((2,)),
            dma((2,)),
        ],
        flops=3 * channels * channels * columns,
        limit=24,
    )(dpre, w_first, grouped)
    half = call(
        add_kernel, shape((ny, nx, nzh * rows, wide), f32), [near] * 3, near
    )(own, keep, other)
    half = lax.all_to_all(half, plane, 0, 0, axis_index_groups=lines(ny, nx))
    blocks = call(
        functools.partial(deal_kernel, ("x", "y")),
        (shape((nzh * rows, wide), f32),) * nx,
        [near],
        (near,) * nx,
    )(half)
    blocks = (blocks[0],) + tuple(
        lax.ppermute(blocks[d], plane, shifts(ny, nx, d)) for d in range(1, nx)
    )
    blocks = call(
        functools.partial(redeal_kernel, "zh"),
        (shape((rows, wide), f32),) * nzh,
        [near] * nx,
        (near,) * nzh,
    )(*blocks)
    blocks = (blocks[0],) + tuple(
        lax.ppermute(blocks[d], "zh", [(i, (i + d) % nzh) for i in range(nzh)])
        for d in range(1, nzh)
    )
    whole = call(spread_kernel, shape((members, rows, wide), f32), [near] * nzh, near)(*blocks)
    whole = lax.all_to_all(whole, ens, 0, 0)
    total_points = columns * lax.axis_size(space)
    factor = 1.0 / math.sqrt(members * total_points)
    w1, b1, w2, b2, loss = call(
        functools.partial(finish_kernel, factor, total_points),
        (
            shape((share, channels), f32),
            shape((1, share), f32),
            shape((share, variables), f32),
            shape((1, variables), f32),
            shape((1, 1), f32),
        ),
        [near],
        (near,) * 5,
        scratch=[pltpu.VMEM((lanes, lanes), f32)],
    )(whole)
    return (loss[0, 0], grad_feat[None], w1, b1[0], w2, b2[0])


def solution(mesh):
    fine = Mesh(mesh.devices.reshape(2, 4, 4, 4, 2), ("zl", "y", "x", "zh", "c"))
    in_specs = (P(ens, None, space), P(None, space), P(space), P(), P(), P(), P(), P(), P())
    out_specs = (P(), P(ens, None, space), P(space, None), P(space), P(space, None), P())
    return jax.shard_map(
        on_device, mesh=fine, in_specs=in_specs, out_specs=out_specs, check_vma=False
    )
```

```python
import functools
import math

import jax
import jax.numpy as jnp
from jax import lax
from jax.experimental import pallas as pl
from jax.experimental.pallas import tpu as pltpu
from jax.sharding import Mesh, PartitionSpec as P

smoothing = 0.0025
loss_scale = 64.0
ens = ("zl", "y")
space = ("x", "zh", "c")
plane = ("y", "x", "c")
lanes = 128
tile = 256
f32, bf16 = jnp.float32, jnp.bfloat16
root = math.sqrt(2.0 / math.pi)
cubic = 0.044715


def dot(a, b, contract):
    return lax.dot_general(a, b, (contract, ((), ())), preferred_element_type=f32)


hbm = pl.BlockSpec(memory_space=pltpu.HBM)
near = pl.BlockSpec(memory_space=pltpu.VMEM)


def call(kernel, out_shape, ins, outs, scratch=(), flops=0, limit=24):
    return pl.pallas_call(
        kernel,
        out_shape=out_shape,
        in_specs=ins,
        out_specs=outs,
        scratch_shapes=scratch,
        compiler_params=pltpu.CompilerParams(vmem_limit_bytes=limit * 2**20),
        cost_estimate=pl.CostEstimate(flops=flops, bytes_accessed=2**22, transcendentals=0),
    )


def columns_of(row, width):
    return jnp.transpose(jnp.broadcast_to(row, (width, row.shape[1])))


def arrive(pairs, sems):
    copies = [pltpu.make_async_copy(s, d, sems.at[i]) for i, (s, d) in enumerate(pairs)]
    for c in copies:
        c.start()
    return copies


def turn(w, wt):
    for j in range(0, w.shape[1], tile):
        wt[j : j + tile, :] = jnp.transpose(w[:, j : j + tile])


def arrive_rows(pairs, count, sems):
    cut = []
    for src, dst in pairs:
        step = src.shape[0] // count
        cut += [(src.at[pl.ds(i * step, step)], dst.at[pl.ds(i * step, step)]) for i in range(count)]
    return arrive(cut, sems)


def turn(w, wt):
    for j in range(0, w.shape[1], tile):
        wt[j : j + tile, :] = jnp.transpose(w[:, j : j + tile])


def forward_kernel(f_hbm, w_hbm, b1_hbm, w2_hbm, b2_hbm, x_ref, f, w, b1, w2, b2, wt, big, small):
    copies = arrive_rows([(w_hbm, w), (f_hbm, f)], 4, big)
    copies += arrive([(b1_hbm, b1), (w2_hbm, w2), (b2_hbm, b2)], small)
    for c in copies:
        c.wait()
    turn(w, wt)
    shift = columns_of(b1[...], lanes)
    bias = columns_of(b2[...], lanes)
    pre = dot(wt[...], f[...], ((1,), (0,))) + jnp.tile(shift, (1, f.shape[1] // lanes))
    t = jnp.tanh(pre * (root + (root * cubic) * (pre * pre)))
    z = (0.5 * pre * (1.0 + t)).astype(bf16)
    x = dot(w2[...], z, ((1,), (0,)))
    for m in range(x_ref.shape[0]):
        x_ref[m] = x[:, m * lanes : (m + 1) * lanes] + bias


def again_kernel(x_hbm, f_hbm, w_hbm, b1_hbm, z_hbm, g_hbm, done_ref, f, w, b1, wt, z, g, big, small, outs):
    copies = arrive_rows([(w_hbm, w), (f_hbm, f)], 4, big) + arrive([(b1_hbm, b1)], small)
    for c in copies:
        c.wait()
    done_ref[...] = jnp.zeros_like(done_ref)
    turn(w, wt)
    half = f.shape[1] // 2
    shift = jnp.tile(columns_of(b1[...], lanes), (1, half // lanes))
    sent = []
    for k in range(2):
        here = pl.ds(k * half, half)
        pre = dot(wt[...], f[:, here], ((1,), (0,))) + shift
        square = pre * pre
        t = jnp.tanh(pre * (root + (root * cubic) * square))
        z[:, here] = (0.5 * pre * (1.0 + t)).astype(bf16)
        inner = root + (3.0 * root * cubic) * square
        g[:, here] = (0.5 * ((1.0 + t) + (pre * inner) * (1.0 - t * t))).astype(bf16)
        for i, (src, dst) in enumerate(((z, z_hbm), (g, g_hbm))):
            c = pltpu.make_async_copy(src.at[:, here], dst.at[:, here], outs.at[k, i])
            c.start()
            sent.append(c)
    for c in sent:
        c.wait()


def pair_kernel(
    done_ref, x_ref, goal_hbm, index_hbm, table_hbm, weight_hbm, dx_ref, misc_ref,
    col, goal_ref, index_ref, table_ref, weight_ref, sems,
):
    members, variables, slab = x_ref.shape
    me = lax.axis_index(ens)
    here = pl.ds(pl.multiple_of(me * slab, slab), slab)
    rows = table_ref.shape[1]
    copies = arrive(
        [
            (index_hbm, index_ref),
            (table_hbm, table_ref),
            (weight_hbm, weight_ref),
            (goal_hbm.at[:, here], goal_ref),
        ],
        sems,
    )
    fields = [x_ref[m] for m in range(members)]
    pull = [None] * members
    spread = None
    for a in range(members):
        for b in range(a + 1, members):
            d = fields[a] - fields[b]
            square = d * d + smoothing
            inverse = lax.rsqrt(square)
            spread = square * inverse if spread is None else spread + square * inverse
            term = d * inverse
            pull[a] = term if pull[a] is None else pull[a] + term
            pull[b] = -term if pull[b] is None else pull[b] - term
    spread = 2.0 * spread + members * math.sqrt(smoothing)
    for c in copies:
        c.wait()
    hot = lax.broadcasted_iota(jnp.int32, (rows, slab), 0) == index_ref[:, here]
    area = lax.dot_general(
        table_ref[...],
        hot.astype(f32),
        (((1,), (0,)), ((), ())),
        precision=lax.Precision.HIGHEST,
        preferred_element_type=f32,
    )
    coef = columns_of(weight_ref[...], slab) * area
    goal = goal_ref[...]
    pairs = members * (members - 1)
    skills = None
    total = None
    for m in range(members):
        miss = fields[m] - goal
        square = miss * miss + smoothing
        inverse = lax.rsqrt(square)
        skills = square * inverse if skills is None else skills + square * inverse
        slope = miss * inverse * (1.0 / members) - pull[m] * (1.0 / pairs)
        grad = (loss_scale * coef * slope).astype(bf16).astype(f32)
        dx_ref[m] = grad
        total = grad if total is None else total + grad
    crps = coef * (skills * (1.0 / members) - spread * (0.5 / pairs))
    col[...] = jnp.zeros_like(col)
    col[:variables, :] = jnp.broadcast_to(jnp.sum(total, axis=1, keepdims=True), (variables, lanes))
    loss = jnp.sum(jnp.sum(crps, axis=0, keepdims=True), axis=1, keepdims=True)
    col[variables : variables + 1, :] = jnp.broadcast_to(loss, (1, lanes))
    share = misc_ref.shape[0]
    lane = lax.broadcasted_iota(jnp.int32, (share, lanes), 1)
    out = jnp.zeros((share, lanes), f32)
    for g in range(lanes // share):
        out = jnp.where(lane == variables + 1 + g, col[g * share : (g + 1) * share, :], out)
    misc_ref[...] = out


def scatter_rows(first, put, nx, nzh, ny, rows):
    for y in range(ny):
        for zh in range(nzh):
            for x in range(nx):
                r = ((x * nzh + zh) * ny + y) * rows
                put(y, x, zh, first[r : r + rows])


def send_kernel(
    back_ref, w2_ref, misc_ref, g_ref, z_ref, f_ref, dpre_ref, send_ref, keep_ref, dx, piece
):
    members, variables, slab = back_ref.shape
    ny, nx, nzh, rows, _ = send_ref.shape
    channels, points = z_ref.shape
    share = ny * rows
    core = lax.axis_index("c")
    dx[...] = jnp.zeros_like(dx)
    for m in range(members):
        dx[:variables, m * slab : (m + 1) * slab] = back_ref[m].astype(bf16)
    lane = lax.broadcasted_iota(jnp.int32, (tile, lanes), 1)
    extra = jnp.tile(misc_ref[...], (tile // share, 1))
    half = f_ref[:, 1 - core].reshape(nx * nzh * share, points)
    for j in range(channels // tile):
        here = slice(j * tile, (j + 1) * tile)
        dz = dot(jnp.transpose(w2_ref[:, here]), dx[:variables, :], ((1,), (0,)))
        d = (dz * g_ref[here, :].astype(f32)).astype(bf16)
        dpre_ref[here, :] = d
        sums = jnp.sum(d.astype(f32), axis=1, keepdims=True)
        second = dot(z_ref[here, :], dx[...], ((1,), (1,)))
        second = jnp.where(lane == variables, sums, second + extra)
        piece[...] = second.reshape(nzh, 2, share, lanes)
        go, stay = piece[:, 1 - core], piece[:, core]
        first = dot(half, d, ((1,), (1,)))
        for y in range(ny):
            for zh in range(nzh):
                send_ref[y, j, zh, :, channels:] = go[zh, y * rows : (y + 1) * rows]
                keep_ref[y, j, zh] = stay[zh, y * rows : (y + 1) * rows]

        def put(y, x, zh, value):
            send_ref[y, x, zh, :, here] = value

        scatter_rows(first, put, nx, nzh, ny, rows)


def window_kernel(d_ref, w_ref, f_ref, own_ref, grad_hbm, grad, outs):
    ny, nx, nzh, rows, channels = own_ref.shape
    core = lax.axis_index("c")
    sent = []
    side = channels // 2
    for k in range(2):
        here = pl.ds(k * side, side)
        grad[here, :] = dot(w_ref[here, :], d_ref[...], ((1,), (0,))).astype(bf16)
        c = pltpu.make_async_copy(grad.at[here, :], grad_hbm.at[here, :], outs.at[k])
        c.start()
        sent.append(c)
    half = f_ref[:, core].reshape(nx * nzh * ny * rows, d_ref.shape[1])
    first = dot(half, d_ref[...], ((1,), (1,)))

    def put(y, x, zh, value):
        own_ref[y, x, zh] = value

    scatter_rows(first, put, nx, nzh, ny, rows)
    for c in sent:
        c.wait()


def add_kernel(own_ref, keep_ref, other_ref, out_ref):
    ny, nx, nzh, rows, channels = own_ref.shape
    core = lax.axis_index("c")
    for y in range(ny):
        for x in range(nx):
            a = jnp.where(core == 0, y, x)
            b = jnp.where(core == 0, x, y)
            for zh in range(nzh):
                here = pl.ds(zh * rows, rows)
                out_ref[a, b, here, :channels] = (
                    own_ref[y, x, zh] + other_ref[y, x, zh, :, :channels]
                )
                out_ref[a, b, here, channels:] = (
                    keep_ref[y, x, zh] + other_ref[y, x, zh, :, channels:]
                )


def deal_kernel(axes, in_ref, *out_refs):
    core = lax.axis_index("c")
    me = jnp.where(core == 0, lax.axis_index(axes[0]), lax.axis_index(axes[1]))
    n = len(out_refs)
    for d in range(n):
        k = lax.rem(me + d, n)
        total = in_ref[0, k]
        for i in range(1, in_ref.shape[0]):
            total = total + in_ref[i, k]
        out_refs[d][...] = total


def redeal_kernel(axis, *refs):
    n = len(refs) // 2
    me = lax.axis_index(axis)
    rows = refs[n].shape[0]
    for d in range(n):
        here = pl.ds(pl.multiple_of(lax.rem(me + d, n) * rows, rows), rows)
        total = refs[0][here, :]
        for i in range(1, n):
            total = total + refs[i][here, :]
        refs[n + d][...] = total


def spread_kernel(*refs):
    out_ref = refs[-1]
    total = refs[0][...]
    for r in refs[1:-1]:
        total = total + r[...]
    for i in range(out_ref.shape[0]):
        out_ref[i] = total


def finish_kernel(factor, points, in_ref, w1_ref, b1_ref, w2_ref, b2_ref, loss_ref, part):
    ny = in_ref.shape[0] // 2
    rows = in_ref.shape[1]
    share, channels = w1_ref.shape
    variables = w2_ref.shape[1]
    part[...] = jnp.zeros_like(part)
    for y in range(ny):
        here = slice(y * rows, (y + 1) * rows)
        w1_ref[here, :] = (in_ref[y, :, :channels] + in_ref[ny + y, :, :channels]) * factor
        part[here, :] = in_ref[y, :, channels:] + in_ref[ny + y, :, channels:]
    w2_ref[...] = part[:share, :variables] * factor
    turned = jnp.transpose(part[...])
    b1_ref[...] = turned[variables : variables + 1, :share] * factor
    line = turned[variables + 1 : variables + 2, :]
    for g in range(1, lanes // share):
        line = line + pltpu.roll(turned[variables + 1 + g : variables + 2 + g, :], g * share, 1)
    b2_ref[...] = line[:, :variables] * factor
    loss_ref[...] = line[:, variables : variables + 1] * (1.0 / points)


def lines(ny, nx):
    at = lambda y, x, c: (y * nx + x) * 2 + c
    down = [[at(y, x, 0) for y in range(ny)] for x in range(nx)]
    along = [[at(y, x, 1) for x in range(nx)] for y in range(ny)]
    return down + along


def shifts(ny, nx, d):
    at = lambda y, x, c: (y * nx + x) * 2 + c
    pairs = [(at(y, x, 0), at(y, (x + d) % nx, 0)) for y in range(ny) for x in range(nx)]
    return pairs + [(at(y, x, 1), at((y + d) % ny, x, 1)) for y in range(ny) for x in range(nx)]


def on_device(
    hidden, target, area_index, area_table, var_weight, w_first, b_first, w_second, b_second
):
    members = lax.axis_size(ens)
    columns = hidden.shape[2]
    variables = target.shape[0]
    channels = w_first.shape[0]
    slab = columns // members
    nx, nzh, nc, ny = (lax.axis_size(a) for a in ("x", "zh", "c", "y"))
    share = channels // (nx * nzh * nc)
    rows = share // ny
    wide = channels + lanes
    shape = jax.ShapeDtypeStruct
    features = hidden[0]
    grouped = features.reshape(nx * nzh, nc, share, columns)
    w2t = w_second.T
    square = (channels, columns)
    dma = pltpu.SemaphoreType.DMA
    mine = call(
        forward_kernel,
        shape((members, variables, slab), f32),
        [hbm] * 5,
        near,
        scratch=[
            pltpu.VMEM(square, bf16),
            pltpu.VMEM((channels, channels), bf16),
            pltpu.VMEM((1, channels), f32),
            pltpu.VMEM((variables, channels), bf16),
            pltpu.VMEM((1, variables), f32),
            pltpu.VMEM((channels, channels), bf16),
            dma((8,)),
            dma((3,)),
        ],
        flops=2 * channels * channels * columns,
        limit=60,
    )(features, w_first, b_first[None], w2t, b_second[None])
    fields = lax.all_to_all(mine, ens, 0, 0)
    z, g, done = call(
        again_kernel,
        (shape(square, bf16), shape(square, bf16), shape((8, lanes), f32)),
        [pl.BlockSpec(memory_space=pl.ANY)] + [hbm] * 3,
        (hbm, hbm, near),
        scratch=[
            pltpu.VMEM(square, bf16),
            pltpu.VMEM((channels, channels), bf16),
            pltpu.VMEM((1, channels), f32),
            pltpu.VMEM((channels, channels), bf16),
            pltpu.VMEM(square, bf16),
            pltpu.VMEM(square, bf16),
            dma((8,)),
            dma((1,)),
            dma((2, 2)),
        ],
        flops=2 * channels * channels * columns,
        limit=60,
    )(mine, features, w_first, b_first[None])
    dx, misc = call(
        pair_kernel,
        (shape((members, variables, slab), f32), shape((share, lanes), f32)),
        [near] * 2 + [hbm] * 4,
        (near, near),
        scratch=[
            pltpu.VMEM((lanes, lanes), f32),
            pltpu.VMEM((variables, slab), f32),
            pltpu.VMEM((1, columns), jnp.int32),
            pltpu.VMEM((1, area_table.shape[0]), f32),
            pltpu.VMEM((1, variables), f32),
            dma((4,)),
        ],
        flops=2**34,
    )(done, fields, target, area_index[None], area_table[None], var_weight[None])
    back = lax.all_to_all(dx, ens, 0, 0)
    part = (ny, nx, nzh, rows)
    dpre, send, keep = call(
        send_kernel,
        (shape(square, bf16), shape(part + (wide,), f32), shape(part + (lanes,), f32)),
        [near] * 6,
        (near, near, near),
        scratch=[pltpu.VMEM((lanes, columns), bf16), pltpu.VMEM((nzh, nc, share, lanes), f32)],
        flops=channels * channels * columns,
        limit=24,
    )(back, w2t, misc, g, z, grouped)
    other = lax.ppermute(send, "c", [(0, 1), (1, 0)])
    own, grad_feat = call(
        window_kernel,
        (shape(part + (channels,), f32), shape(square, bf16)),
        [near] * 3,
        (near, hbm),
        scratch=[pltpu.VMEM(square, bf16), dma((2,))],
        flops=3 * channels * channels * columns,
        limit=24,
    )(dpre, w_first, grouped)
    half = call(
        add_kernel, shape((ny, nx, nzh * rows, wide), f32), [near] * 3, near
    )(own, keep, other)
    half = lax.all_to_all(half, plane, 0, 0, axis_index_groups=lines(ny, nx))
    blocks = call(
        functools.partial(deal_kernel, ("x", "y")),
        (shape((nzh * rows, wide), f32),) * nx,
        [near],
        (near,) * nx,
    )(half)
    blocks = (blocks[0],) + tuple(
        lax.ppermute(blocks[d], plane, shifts(ny, nx, d)) for d in range(1, nx)
    )
    blocks = call(
        functools.partial(redeal_kernel, "zh"),
        (shape((rows, wide), f32),) * nzh,
        [near] * nx,
        (near,) * nzh,
    )(*blocks)
    blocks = (blocks[0],) + tuple(
        lax.ppermute(blocks[d], "zh", [(i, (i + d) % nzh) for i in range(nzh)])
        for d in range(1, nzh)
    )
    whole = call(spread_kernel, shape((members, rows, wide), f32), [near] * nzh, near)(*blocks)
    whole = lax.all_to_all(whole, ens, 0, 0)
    total_points = columns * lax.axis_size(space)
    factor = 1.0 / math.sqrt(members * total_points)
    w1, b1, w2, b2, loss = call(
        functools.partial(finish_kernel, factor, total_points),
        (
            shape((share, channels), f32),
            shape((1, share), f32),
            shape((share, variables), f32),
            shape((1, variables), f32),
            shape((1, 1), f32),
        ),
        [near],
        (near,) * 5,
        scratch=[pltpu.VMEM((lanes, lanes), f32)],
    )(whole)
    return (loss[0, 0], grad_feat[None], w1, b1[0], w2, b2[0])


def solution(mesh):
    fine = Mesh(mesh.devices.reshape(2, 4, 4, 4, 2), ("zl", "y", "x", "zh", "c"))
    in_specs = (P(ens, None, space), P(None, space), P(space), P(), P(), P(), P(), P(), P())
    out_specs = (P(), P(ens, None, space), P(space, None), P(space), P(space, None), P())
    return jax.shard_map(
        on_device, mesh=fine, in_specs=in_specs, out_specs=out_specs, check_vma=False
    )
```

```python
import functools
import math

import jax
import jax.numpy as jnp
from jax import lax
from jax.experimental import pallas as pl
from jax.experimental.pallas import tpu as pltpu
from jax.sharding import Mesh, PartitionSpec as P

smoothing = 0.0025
loss_scale = 64.0
ens = ("zl", "y")
space = ("x", "zh", "c")
plane = ("y", "x", "c")
lanes = 128
tile = 256
f32, bf16 = jnp.float32, jnp.bfloat16
root = math.sqrt(2.0 / math.pi)
cubic = 0.044715


def dot(a, b, contract):
    return lax.dot_general(a, b, (contract, ((), ())), preferred_element_type=f32)


hbm = pl.BlockSpec(memory_space=pltpu.HBM)
near = pl.BlockSpec(memory_space=pltpu.VMEM)


def call(kernel, out_shape, ins, outs, scratch=(), flops=0, limit=24):
    return pl.pallas_call(
        kernel,
        out_shape=out_shape,
        in_specs=ins,
        out_specs=outs,
        scratch_shapes=scratch,
        compiler_params=pltpu.CompilerParams(vmem_limit_bytes=limit * 2**20),
        cost_estimate=pl.CostEstimate(flops=flops, bytes_accessed=2**22, transcendentals=0),
    )


def columns_of(row, width):
    return jnp.transpose(jnp.broadcast_to(row, (width, row.shape[1])))


def arrive(pairs, sems):
    copies = [pltpu.make_async_copy(s, d, sems.at[i]) for i, (s, d) in enumerate(pairs)]
    for c in copies:
        c.start()
    return copies


def turn(w, wt):
    for j in range(0, w.shape[1], tile):
        wt[j : j + tile, :] = jnp.transpose(w[:, j : j + tile])


def arrive_rows(pairs, count, sems):
    cut = []
    for src, dst in pairs:
        step = src.shape[0] // count
        cut += [(src.at[pl.ds(i * step, step)], dst.at[pl.ds(i * step, step)]) for i in range(count)]
    return arrive(cut, sems)


def turn(w, wt):
    for j in range(0, w.shape[1], tile):
        wt[j : j + tile, :] = jnp.transpose(w[:, j : j + tile])


def forward_kernel(f_hbm, w_hbm, b1_hbm, w2_hbm, b2_hbm, x_ref, f, w, b1, w2, b2, wt, big, small):
    copies = arrive_rows([(w_hbm, w), (f_hbm, f)], 4, big)
    copies += arrive([(b1_hbm, b1), (w2_hbm, w2), (b2_hbm, b2)], small)
    for c in copies:
        c.wait()
    turn(w, wt)
    shift = columns_of(b1[...], lanes)
    bias = columns_of(b2[...], lanes)
    pre = dot(wt[...], f[...], ((1,), (0,))) + jnp.tile(shift, (1, f.shape[1] // lanes))
    t = jnp.tanh(pre * (root + (root * cubic) * (pre * pre)))
    z = (0.5 * pre * (1.0 + t)).astype(bf16)
    x = dot(w2[...], z, ((1,), (0,)))
    for m in range(x_ref.shape[0]):
        x_ref[m] = x[:, m * lanes : (m + 1) * lanes] + bias


def again_kernel(x_hbm, f_hbm, w_hbm, b1_hbm, z_hbm, g_hbm, done_ref, f, w, b1, wt, z, g, big, small, outs):
    copies = arrive_rows([(w_hbm, w), (f_hbm, f)], 4, big) + arrive([(b1_hbm, b1)], small)
    for c in copies:
        c.wait()
    done_ref[...] = jnp.zeros_like(done_ref)
    turn(w, wt)
    half = f.shape[1] // 2
    shift = jnp.tile(columns_of(b1[...], lanes), (1, half // lanes))
    sent = []
    for k in range(2):
        here = pl.ds(k * half, half)
        pre = dot(wt[...], f[:, here], ((1,), (0,))) + shift
        square = pre * pre
        rise = 0.5 + 0.5 * jnp.tanh(pre * (root + (root * cubic) * square))
        z[:, here] = (pre * rise).astype(bf16)
        inner = 2.0 * root + (6.0 * root * cubic) * square
        g[:, here] = (rise + (pre * inner) * (rise * (1.0 - rise))).astype(bf16)
        for i, (src, dst) in enumerate(((z, z_hbm), (g, g_hbm))):
            c = pltpu.make_async_copy(src.at[:, here], dst.at[:, here], outs.at[k, i])
            c.start()
            sent.append(c)
    for c in sent:
        c.wait()


def pair_kernel(
    done_ref, x_ref, goal_hbm, index_hbm, table_hbm, weight_hbm, dx_ref, misc_ref,
    col, goal_ref, index_ref, table_ref, weight_ref, sems,
):
    members, variables, slab = x_ref.shape
    me = lax.axis_index(ens)
    here = pl.ds(pl.multiple_of(me * slab, slab), slab)
    rows = table_ref.shape[0]
    copies = arrive(
        [
            (index_hbm, index_ref),
            (table_hbm, table_ref),
            (weight_hbm, weight_ref),
            (goal_hbm.at[:, here], goal_ref),
        ],
        sems,
    )
    fields = [x_ref[m] for m in range(members)]
    pull = [None] * members
    spread = None
    for a in range(members):
        for b in range(a + 1, members):
            d = fields[a] - fields[b]
            square = d * d + smoothing
            inverse = lax.rsqrt(square)
            spread = square * inverse if spread is None else spread + square * inverse
            term = d * inverse
            pull[a] = term if pull[a] is None else pull[a] + term
            pull[b] = -term if pull[b] is None else pull[b] - term
    spread = 2.0 * spread + members * math.sqrt(smoothing)
    for c in copies:
        c.wait()
    hot = lax.broadcasted_iota(jnp.int32, (rows, slab), 0) == index_ref[:, here]
    area = lax.dot_general(
        table_ref[...].reshape(1, rows),
        hot.astype(f32),
        (((1,), (0,)), ((), ())),
        precision=lax.Precision.HIGHEST,
        preferred_element_type=f32,
    )
    coef = columns_of(weight_ref[...], slab) * area
    goal = goal_ref[...]
    pairs = members * (members - 1)
    skills = None
    total = None
    for m in range(members):
        miss = fields[m] - goal
        square = miss * miss + smoothing
        inverse = lax.rsqrt(square)
        skills = square * inverse if skills is None else skills + square * inverse
        slope = miss * inverse * (1.0 / members) - pull[m] * (1.0 / pairs)
        grad = (loss_scale * coef * slope).astype(bf16).astype(f32)
        dx_ref[m] = grad
        total = grad if total is None else total + grad
    crps = coef * (skills * (1.0 / members) - spread * (0.5 / pairs))
    col[...] = jnp.zeros_like(col)
    col[:variables, :] = jnp.broadcast_to(jnp.sum(total, axis=1, keepdims=True), (variables, lanes))
    loss = jnp.sum(jnp.sum(crps, axis=0, keepdims=True), axis=1, keepdims=True)
    col[variables : variables + 1, :] = jnp.broadcast_to(loss, (1, lanes))
    share = misc_ref.shape[0]
    lane = lax.broadcasted_iota(jnp.int32, (share, lanes), 1)
    out = jnp.zeros((share, lanes), f32)
    for g in range(lanes // share):
        out = jnp.where(lane == variables + 1 + g, col[g * share : (g + 1) * share, :], out)
    misc_ref[...] = out


def scatter_rows(first, put, nx, nzh, ny, rows):
    for y in range(ny):
        for zh in range(nzh):
            for x in range(nx):
                r = ((x * nzh + zh) * ny + y) * rows
                put(y, x, zh, first[r : r + rows])


def gradient_rows(w2_ref, g_ref, dx, here):
    dz = dot(jnp.transpose(w2_ref[:, here]), dx, ((1,), (0,)))
    return (dz * g_ref[here, :].astype(f32)).astype(bf16)


def first_kernel(back_ref, w2_ref, g_ref, f_ref, d_ref, dx_ref, send_ref):
    members, variables, slab = back_ref.shape
    ny, nx, nzh, rows, wide = send_ref.shape
    core = lax.axis_index("c")
    dx_ref[...] = jnp.zeros_like(dx_ref)
    for m in range(members):
        dx_ref[:variables, m * slab : (m + 1) * slab] = back_ref[m].astype(bf16)
    half = f_ref[:, 1 - core].reshape(nx * nzh * ny * rows, dx_ref.shape[1])
    for j in range(wide // tile):
        here = slice(j * tile, (j + 1) * tile)
        d = gradient_rows(w2_ref, g_ref, dx_ref[:variables, :], here)
        d_ref[here, :] = d
        first = dot(half, d, ((1,), (1,)))

        def put(y, x, zh, value):
            send_ref[y, x, zh, :, here] = value

        scatter_rows(first, put, nx, nzh, ny, rows)


def second_kernel(
    d1_ref, dx_ref, w2_ref, misc_ref, g_ref, z_ref, f_ref, d_ref, send_ref, keep_ref, piece
):
    ny, nx, nzh, rows, wide = send_ref.shape
    wide = wide - lanes
    variables = w2_ref.shape[0]
    channels, points = z_ref.shape
    share = ny * rows
    core = lax.axis_index("c")
    half = f_ref[:, 1 - core].reshape(nx * nzh * share, points)
    base = channels - wide
    for j in range(wide // tile):
        here = slice(j * tile, (j + 1) * tile)
        there = slice(base + j * tile, base + (j + 1) * tile)
        d = gradient_rows(w2_ref, g_ref, dx_ref[:variables, :], there)
        d_ref[here, :] = d
        first = dot(half, d, ((1,), (1,)))

        def put(y, x, zh, value):
            send_ref[y, x, zh, :, here] = value

        scatter_rows(first, put, nx, nzh, ny, rows)
    lane = lax.broadcasted_iota(jnp.int32, (tile, lanes), 1)
    extra = jnp.tile(misc_ref[...], (tile // share, 1))
    for j in range(channels // tile):
        here = slice(j * tile, (j + 1) * tile)
        d = d1_ref[here, :] if j * tile < base else d_ref[j * tile - base : (j + 1) * tile - base, :]
        sums = jnp.sum(d.astype(f32), axis=1, keepdims=True)
        second = dot(z_ref[here, :], dx_ref[...], ((1,), (1,)))
        second = jnp.where(lane == variables, sums, second + extra)
        piece[...] = second.reshape(nzh, 2, share, lanes)
        go, stay = piece[:, 1 - core], piece[:, core]
        for y in range(ny):
            for zh in range(nzh):
                send_ref[y, j, zh, :, wide:] = go[zh, y * rows : (y + 1) * rows]
                keep_ref[y, j, zh] = stay[zh, y * rows : (y + 1) * rows]


def after_kernel(left_ref, right_ref, out_ref):
    pass


def own_kernel(d1_ref, d2_ref, f_ref, left_ref, own_ref):
    ny, nx, nzh, rows, channels = own_ref.shape
    core = lax.axis_index("c")
    cut, points = d1_ref.shape
    half = f_ref[:, core].reshape(nx * nzh * ny * rows, points)
    for j in range(channels // tile):
        here = slice(j * tile, (j + 1) * tile)
        early = j * tile < cut
        d = d1_ref[here, :] if early else d2_ref[j * tile - cut : (j + 1) * tile - cut, :]
        first = dot(half, d, ((1,), (1,)))

        def put(y, x, zh, value):
            own_ref[y, x, zh, :, here] = value + left_ref[y, x, zh, :, here] if early else value

        scatter_rows(first, put, nx, nzh, ny, rows)


def grad_kernel(late_ref, d1_ref, d2_ref, w_ref, grad_hbm, done_ref, d, grad, outs):
    done_ref[...] = jnp.zeros_like(done_ref)
    channels = w_ref.shape[0]
    split = d1_ref.shape[0]
    d[:split, :] = d1_ref[...]
    d[split:, :] = d2_ref[...]
    sent = []
    side = channels // 2
    for k in range(2):
        here = pl.ds(k * side, side)
        grad[here, :] = dot(w_ref[here, :], d[...], ((1,), (0,))).astype(bf16)
        c = pltpu.make_async_copy(grad.at[here, :], grad_hbm.at[here, :], outs.at[k])
        c.start()
        sent.append(c)
    for c in sent:
        c.wait()


def add_kernel(own_ref, keep_ref, right_ref, out_ref):
    ny, nx, nzh, rows, channels = own_ref.shape
    width = right_ref.shape[4] - keep_ref.shape[4]
    cut = channels - width
    core = lax.axis_index("c")
    for y in range(ny):
        for x in range(nx):
            a = jnp.where(core == 0, y, x)
            b = jnp.where(core == 0, x, y)
            for zh in range(nzh):
                here = pl.ds(zh * rows, rows)
                out_ref[a, b, here, :cut] = own_ref[y, x, zh, :, :cut]
                out_ref[a, b, here, cut:channels] = (
                    own_ref[y, x, zh, :, cut:] + right_ref[y, x, zh, :, :width]
                )
                out_ref[a, b, here, channels:] = (
                    keep_ref[y, x, zh] + right_ref[y, x, zh, :, width:]
                )


def deal_kernel(axes, in_ref, *out_refs):
    core = lax.axis_index("c")
    me = jnp.where(core == 0, lax.axis_index(axes[0]), lax.axis_index(axes[1]))
    n = len(out_refs)
    for d in range(n):
        k = lax.rem(me + d, n)
        total = in_ref[0, k]
        for i in range(1, in_ref.shape[0]):
            total = total + in_ref[i, k]
        out_refs[d][...] = total


def redeal_kernel(axis, done_ref, *refs):
    n = len(refs) // 2
    me = lax.axis_index(axis)
    rows = refs[n].shape[0]
    for d in range(n):
        here = pl.ds(pl.multiple_of(lax.rem(me + d, n) * rows, rows), rows)
        total = refs[0][here, :]
        for i in range(1, n):
            total = total + refs[i][here, :]
        refs[n + d][...] = total


def spread_kernel(*refs):
    out_ref = refs[-1]
    total = refs[0][...]
    for r in refs[1:-1]:
        total = total + r[...]
    for i in range(out_ref.shape[0]):
        out_ref[i] = total


def finish_kernel(factor, points, in_ref, w1_ref, b1_ref, w2_ref, b2_ref, loss_ref, part):
    ny = in_ref.shape[0] // 2
    rows = in_ref.shape[1]
    share, channels = w1_ref.shape
    variables = w2_ref.shape[1]
    part[...] = jnp.zeros_like(part)
    for y in range(ny):
        here = slice(y * rows, (y + 1) * rows)
        w1_ref[here, :] = (in_ref[y, :, :channels] + in_ref[ny + y, :, :channels]) * factor
        part[here, :] = in_ref[y, :, channels:] + in_ref[ny + y, :, channels:]
    w2_ref[...] = part[:share, :variables] * factor
    turned = jnp.transpose(part[...])
    b1_ref[...] = turned[variables : variables + 1, :share] * factor
    line = turned[variables + 1 : variables + 2, :]
    for g in range(1, lanes // share):
        line = line + pltpu.roll(turned[variables + 1 + g : variables + 2 + g, :], g * share, 1)
    b2_ref[...] = line[:, :variables] * factor
    loss_ref[...] = line[:, variables : variables + 1] * (1.0 / points)


def lines(ny, nx):
    at = lambda y, x, c: (y * nx + x) * 2 + c
    down = [[at(y, x, 0) for y in range(ny)] for x in range(nx)]
    along = [[at(y, x, 1) for x in range(nx)] for y in range(ny)]
    return down + along


def shifts(ny, nx, d):
    at = lambda y, x, c: (y * nx + x) * 2 + c
    pairs = [(at(y, x, 0), at(y, (x + d) % nx, 0)) for y in range(ny) for x in range(nx)]
    return pairs + [(at(y, x, 1), at((y + d) % ny, x, 1)) for y in range(ny) for x in range(nx)]


def on_device(
    hidden, target, area_index, area_table, var_weight, w_first, b_first, w_second, b_second
):
    members = lax.axis_size(ens)
    columns = hidden.shape[2]
    variables = target.shape[0]
    channels = w_first.shape[0]
    slab = columns // members
    nx, nzh, nc, ny = (lax.axis_size(a) for a in ("x", "zh", "c", "y"))
    share = channels // (nx * nzh * nc)
    rows = share // ny
    wide = channels + lanes
    shape = jax.ShapeDtypeStruct
    features = hidden[0]
    grouped = features.reshape(nx * nzh, nc, share, columns)
    w2t = w_second.T
    square = (channels, columns)
    dma = pltpu.SemaphoreType.DMA
    mine = call(
        forward_kernel,
        shape((members, variables, slab), f32),
        [hbm] * 5,
        near,
        scratch=[
            pltpu.VMEM(square, bf16),
            pltpu.VMEM((channels, channels), bf16),
            pltpu.VMEM((1, channels), f32),
            pltpu.VMEM((variables, channels), bf16),
            pltpu.VMEM((1, variables), f32),
            pltpu.VMEM((channels, channels), bf16),
            dma((8,)),
            dma((3,)),
        ],
        flops=2 * channels * channels * columns,
        limit=60,
    )(features, w_first, b_first[None], w2t, b_second[None])
    fields = lax.all_to_all(mine, ens, 0, 0)
    z, g, done = call(
        again_kernel,
        (shape(square, bf16), shape(square, bf16), shape((8, lanes), f32)),
        [pl.BlockSpec(memory_space=pl.ANY)] + [hbm] * 3,
        (hbm, hbm, near),
        scratch=[
            pltpu.VMEM(square, bf16),
            pltpu.VMEM((channels, channels), bf16),
            pltpu.VMEM((1, channels), f32),
            pltpu.VMEM((channels, channels), bf16),
            pltpu.VMEM(square, bf16),
            pltpu.VMEM(square, bf16),
            dma((8,)),
            dma((1,)),
            dma((2, 2)),
        ],
        flops=2 * channels * channels * columns,
        limit=60,
    )(mine, features, w_first, b_first[None])
    dx, misc = call(
        pair_kernel,
        (shape((members, variables, slab), f32), shape((share, lanes), f32)),
        [near] * 2 + [hbm] * 4,
        (near, near),
        scratch=[
            pltpu.VMEM((lanes, lanes), f32),
            pltpu.VMEM((variables, slab), f32),
            pltpu.VMEM((1, columns), jnp.int32),
            pltpu.VMEM(area_table.shape, f32),
            pltpu.VMEM((1, variables), f32),
            dma((4,)),
        ],
        flops=2**34,
    )(done, fields, target, area_index[None], area_table, var_weight[None])
    back = lax.all_to_all(dx, ens, 0, 0)
    part = (ny, nx, nzh, rows)
    cut = channels // 2
    mirror = [(0, 1), (1, 0)]
    d1, dxs, left = call(
        first_kernel,
        (shape((cut, columns), bf16), shape((lanes, columns), bf16), shape(part + (cut,), f32)),
        [near] * 4,
        (near,) * 3,
        flops=channels * channels * columns // 2,
    )(back, w2t, g, grouped)
    left = lax.ppermute(left, "c", mirror)
    d2, right, keep = call(
        second_kernel,
        (
            shape((channels - cut, columns), bf16),
            shape(part + (channels - cut + lanes,), f32),
            shape(part + (lanes,), f32),
        ),
        [near] * 7,
        (near,) * 3,
        scratch=[pltpu.VMEM((nzh, nc, share, lanes), f32)],
        flops=channels * channels * columns // 2,
    )(d1, dxs, w2t, misc, g, z, grouped)
    right = pl.pallas_call(
        after_kernel,
        out_shape=shape(right.shape, f32),
        in_specs=[pl.BlockSpec(memory_space=pl.ANY)] * 2,
        out_specs=pl.BlockSpec(memory_space=pl.ANY),
        input_output_aliases={1: 0},
        compiler_params=pltpu.CompilerParams(vmem_limit_bytes=2**20),
    )(left, right)
    right = lax.ppermute(right, "c", mirror)
    own = call(
        own_kernel,
        shape(part + (channels,), f32),
        [near] * 4,
        near,
    )(d1, d2, grouped, left)
    half = call(
        add_kernel, shape((ny, nx, nzh * rows, wide), f32), [near] * 3, near
    )(own, keep, right)
    half = lax.all_to_all(half, plane, 0, 0, axis_index_groups=lines(ny, nx))
    blocks = call(
        functools.partial(deal_kernel, ("x", "y")),
        (shape((nzh * rows, wide), f32),) * nx,
        [near],
        (near,) * nx,
    )(half)
    grad_feat, built = call(
        grad_kernel,
        (shape(square, bf16), shape((8, lanes), f32)),
        [near] * 4,
        (hbm, near),
        scratch=[pltpu.VMEM(square, bf16), pltpu.VMEM(square, bf16), dma((2,))],
        flops=2 * channels * channels * columns,
    )(blocks[0], d1, d2, w_first)
    blocks = (blocks[0],) + tuple(
        lax.ppermute(blocks[d], plane, shifts(ny, nx, d)) for d in range(1, nx)
    )
    blocks = call(
        functools.partial(redeal_kernel, "zh"),
        (shape((rows, wide), f32),) * nzh,
        [near] * (1 + nx),
        (near,) * nzh,
    )(built, *blocks)
    blocks = (blocks[0],) + tuple(
        lax.ppermute(blocks[d], "zh", [(i, (i + d) % nzh) for i in range(nzh)])
        for d in range(1, nzh)
    )
    whole = call(spread_kernel, shape((members, rows, wide), f32), [near] * nzh, near)(*blocks)
    whole = lax.all_to_all(whole, ens, 0, 0)
    total_points = columns * lax.axis_size(space)
    factor = 1.0 / math.sqrt(members * total_points)
    w1, b1, w2, b2, loss = call(
        functools.partial(finish_kernel, factor, total_points),
        (
            shape((share, channels), f32),
            shape((1, share), f32),
            shape((share, variables), f32),
            shape((1, variables), f32),
            shape((1, 1), f32),
        ),
        [near],
        (near,) * 5,
        scratch=[pltpu.VMEM((lanes, lanes), f32)],
    )(whole)
    return (loss[0, 0], grad_feat[None], w1, b1[0], w2, b2[0])


def solution(mesh):
    fine = Mesh(mesh.devices.reshape(2, 4, 4, 4, 2), ("zl", "y", "x", "zh", "c"))
    in_specs = (P(ens, None, space), P(None, space), P(space), P(), P(), P(), P(), P(), P())
    out_specs = (P(), P(ens, None, space), P(space, None), P(space), P(space, None), P())
    return jax.shard_map(
        on_device, mesh=fine, in_specs=in_specs, out_specs=out_specs, check_vma=False
    )
```

```python
import functools
import math

import jax
import jax.numpy as jnp
from jax import lax
from jax.experimental import pallas as pl
from jax.experimental.pallas import tpu as pltpu
from jax.sharding import Mesh, PartitionSpec as P

smoothing = 0.0025
loss_scale = 64.0
ens = ("zl", "y")
space = ("x", "zh", "c")
plane = ("y", "x", "c")
lanes = 128
tile = 256
f32, bf16 = jnp.float32, jnp.bfloat16
root = math.sqrt(2.0 / math.pi)
cubic = 0.044715


def dot(a, b, contract):
    return lax.dot_general(a, b, (contract, ((), ())), preferred_element_type=f32)


hbm = pl.BlockSpec(memory_space=pltpu.HBM)
near = pl.BlockSpec(memory_space=pltpu.VMEM)


def call(kernel, out_shape, ins, outs, scratch=(), flops=0, limit=24):
    return pl.pallas_call(
        kernel,
        out_shape=out_shape,
        in_specs=ins,
        out_specs=outs,
        scratch_shapes=scratch,
        compiler_params=pltpu.CompilerParams(vmem_limit_bytes=limit * 2**20),
        cost_estimate=pl.CostEstimate(flops=flops, bytes_accessed=2**22, transcendentals=0),
    )


def columns_of(row, width):
    return jnp.transpose(jnp.broadcast_to(row, (width, row.shape[1])))


def arrive(pairs, sems):
    copies = [pltpu.make_async_copy(s, d, sems.at[i]) for i, (s, d) in enumerate(pairs)]
    for c in copies:
        c.start()
    return copies


def turn(w, wt):
    for j in range(0, w.shape[1], tile):
        wt[j : j + tile, :] = jnp.transpose(w[:, j : j + tile])


def arrive_rows(pairs, count, sems):
    cut = []
    for src, dst in pairs:
        step = src.shape[0] // count
        cut += [(src.at[pl.ds(i * step, step)], dst.at[pl.ds(i * step, step)]) for i in range(count)]
    return arrive(cut, sems)


def turn(w, wt):
    for j in range(0, w.shape[1], tile):
        wt[j : j + tile, :] = jnp.transpose(w[:, j : j + tile])


def forward_kernel(f_hbm, w_hbm, b1_hbm, w2_hbm, b2_hbm, x_ref, f, w, b1, w2, b2, wt, big, small):
    copies = arrive_rows([(w_hbm, w), (f_hbm, f)], 4, big)
    copies += arrive([(b1_hbm, b1), (w2_hbm, w2), (b2_hbm, b2)], small)
    for c in copies:
        c.wait()
    turn(w, wt)
    shift = columns_of(b1[...], lanes)
    bias = columns_of(b2[...], lanes)
    pre = dot(wt[...], f[...], ((1,), (0,))) + jnp.tile(shift, (1, f.shape[1] // lanes))
    t = jnp.tanh(pre * (root + (root * cubic) * (pre * pre)))
    z = (0.5 * pre * (1.0 + t)).astype(bf16)
    x = dot(w2[...], z, ((1,), (0,)))
    for m in range(x_ref.shape[0]):
        x_ref[m] = x[:, m * lanes : (m + 1) * lanes] + bias


def again_kernel(x_hbm, f_hbm, w_hbm, b1_hbm, z_hbm, g_hbm, done_ref, f, w, b1, wt, z, g, big, small, outs):
    copies = arrive_rows([(w_hbm, w), (f_hbm, f)], 4, big) + arrive([(b1_hbm, b1)], small)
    for c in copies:
        c.wait()
    done_ref[...] = jnp.zeros_like(done_ref)
    turn(w, wt)
    half = f.shape[1] // 2
    shift = jnp.tile(columns_of(b1[...], lanes), (1, half // lanes))
    sent = []
    for k in range(2):
        here = pl.ds(k * half, half)
        pre = dot(wt[...], f[:, here], ((1,), (0,))) + shift
        square = pre * pre
        rise = 0.5 + 0.5 * jnp.tanh(pre * (root + (root * cubic) * square))
        z[:, here] = (pre * rise).astype(bf16)
        inner = 2.0 * root + (6.0 * root * cubic) * square
        g[:, here] = (rise + (pre * inner) * (rise * (1.0 - rise))).astype(bf16)
        for i, (src, dst) in enumerate(((z, z_hbm), (g, g_hbm))):
            c = pltpu.make_async_copy(src.at[:, here], dst.at[:, here], outs.at[k, i])
            c.start()
            sent.append(c)
    for c in sent:
        c.wait()


def pair_kernel(
    done_ref, x_ref, goal_hbm, index_hbm, table_hbm, weight_hbm, dx_ref, misc_ref,
    col, goal_ref, index_ref, table_ref, weight_ref, sems,
):
    members, variables, slab = x_ref.shape
    me = lax.axis_index(ens)
    here = pl.ds(pl.multiple_of(me * slab, slab), slab)
    rows = table_ref.shape[0]
    copies = arrive(
        [
            (index_hbm, index_ref),
            (table_hbm, table_ref),
            (weight_hbm, weight_ref),
            (goal_hbm.at[:, here], goal_ref),
        ],
        sems,
    )
    fields = [x_ref[m] for m in range(members)]
    pull = [None] * members
    spread = None
    for a in range(members):
        for b in range(a + 1, members):
            d = fields[a] - fields[b]
            square = d * d + smoothing
            inverse = lax.rsqrt(square)
            spread = square * inverse if spread is None else spread + square * inverse
            term = d * inverse
            pull[a] = term if pull[a] is None else pull[a] + term
            pull[b] = -term if pull[b] is None else pull[b] - term
    spread = 2.0 * spread + members * math.sqrt(smoothing)
    for c in copies:
        c.wait()
    hot = lax.broadcasted_iota(jnp.int32, (rows, slab), 0) == index_ref[:, here]
    area = lax.dot_general(
        table_ref[...].reshape(1, rows),
        hot.astype(f32),
        (((1,), (0,)), ((), ())),
        precision=lax.Precision.HIGHEST,
        preferred_element_type=f32,
    )
    coef = columns_of(weight_ref[...], slab) * area
    goal = goal_ref[...]
    pairs = members * (members - 1)
    skills = None
    total = None
    for m in range(members):
        miss = fields[m] - goal
        square = miss * miss + smoothing
        inverse = lax.rsqrt(square)
        skills = square * inverse if skills is None else skills + square * inverse
        slope = miss * inverse * (1.0 / members) - pull[m] * (1.0 / pairs)
        grad = (loss_scale * coef * slope).astype(bf16).astype(f32)
        dx_ref[m] = grad
        total = grad if total is None else total + grad
    crps = coef * (skills * (1.0 / members) - spread * (0.5 / pairs))
    col[...] = jnp.zeros_like(col)
    col[:variables, :] = jnp.broadcast_to(jnp.sum(total, axis=1, keepdims=True), (variables, lanes))
    loss = jnp.sum(jnp.sum(crps, axis=0, keepdims=True), axis=1, keepdims=True)
    col[variables : variables + 1, :] = jnp.broadcast_to(loss, (1, lanes))
    share = misc_ref.shape[0]
    lane = lax.broadcasted_iota(jnp.int32, (share, lanes), 1)
    out = jnp.zeros((share, lanes), f32)
    for g in range(lanes // share):
        out = jnp.where(lane == variables + 1 + g, col[g * share : (g + 1) * share, :], out)
    misc_ref[...] = out


def scatter_rows(first, put, nx, nzh, ny, rows):
    for y in range(ny):
        for zh in range(nzh):
            for x in range(nx):
                r = ((x * nzh + zh) * ny + y) * rows
                put(y, x, zh, first[r : r + rows])


def gradient_rows(w2_ref, g_ref, dx, here):
    dz = dot(jnp.transpose(w2_ref[:, here]), dx, ((1,), (0,)))
    return (dz * g_ref[here, :].astype(f32)).astype(bf16)


def first_kernel(back_ref, w2_ref, g_ref, f_ref, d_ref, dx_ref, send_ref):
    members, variables, slab = back_ref.shape
    ny, nx, nzh, rows, wide = send_ref.shape
    core = lax.axis_index("c")
    dx_ref[...] = jnp.zeros_like(dx_ref)
    for m in range(members):
        dx_ref[:variables, m * slab : (m + 1) * slab] = back_ref[m].astype(bf16)
    half = f_ref[:, 1 - core].reshape(nx * nzh * ny * rows, dx_ref.shape[1])
    for j in range(wide // tile):
        here = slice(j * tile, (j + 1) * tile)
        d = gradient_rows(w2_ref, g_ref, dx_ref[:variables, :], here)
        d_ref[here, :] = d
        first = dot(half, d, ((1,), (1,)))

        def put(y, x, zh, value):
            send_ref[y, x, zh, :, here] = value

        scatter_rows(first, put, nx, nzh, ny, rows)


def second_kernel(
    d1_ref, dx_ref, w2_ref, misc_ref, g_ref, z_ref, f_ref, d_ref, send_ref, keep_ref, piece
):
    ny, nx, nzh, rows, wide = send_ref.shape
    wide = wide - lanes
    variables = w2_ref.shape[0]
    channels, points = z_ref.shape
    share = ny * rows
    core = lax.axis_index("c")
    half = f_ref[:, 1 - core].reshape(nx * nzh * share, points)
    base = channels - wide
    for j in range(wide // tile):
        here = slice(j * tile, (j + 1) * tile)
        there = slice(base + j * tile, base + (j + 1) * tile)
        d = gradient_rows(w2_ref, g_ref, dx_ref[:variables, :], there)
        d_ref[here, :] = d
        first = dot(half, d, ((1,), (1,)))

        def put(y, x, zh, value):
            send_ref[y, x, zh, :, here] = value

        scatter_rows(first, put, nx, nzh, ny, rows)
    lane = lax.broadcasted_iota(jnp.int32, (tile, lanes), 1)
    extra = jnp.tile(misc_ref[...], (tile // share, 1))
    for j in range(channels // tile):
        here = slice(j * tile, (j + 1) * tile)
        d = d1_ref[here, :] if j * tile < base else d_ref[j * tile - base : (j + 1) * tile - base, :]
        sums = jnp.sum(d.astype(f32), axis=1, keepdims=True)
        second = dot(z_ref[here, :], dx_ref[...], ((1,), (1,)))
        second = jnp.where(lane == variables, sums, second + extra)
        piece[...] = second.reshape(nzh, 2, share, lanes)
        go, stay = piece[:, 1 - core], piece[:, core]
        for y in range(ny):
            for zh in range(nzh):
                send_ref[y, j, zh, :, wide:] = go[zh, y * rows : (y + 1) * rows]
                keep_ref[y, j, zh] = stay[zh, y * rows : (y + 1) * rows]


def after_kernel(left_ref, right_ref, out_ref):
    pass


def own_kernel(d1_ref, d2_ref, f_ref, left_ref, own_ref):
    ny, nx, nzh, rows, channels = own_ref.shape
    core = lax.axis_index("c")
    cut, points = d1_ref.shape
    half = f_ref[:, core].reshape(nx * nzh * ny * rows, points)
    for j in range(channels // tile):
        here = slice(j * tile, (j + 1) * tile)
        early = j * tile < cut
        d = d1_ref[here, :] if early else d2_ref[j * tile - cut : (j + 1) * tile - cut, :]
        first = dot(half, d, ((1,), (1,)))

        def put(y, x, zh, value):
            own_ref[y, x, zh, :, here] = value + left_ref[y, x, zh, :, here] if early else value

        scatter_rows(first, put, nx, nzh, ny, rows)


def grad_kernel(late_ref, d1_ref, d2_ref, w_ref, grad_hbm, done_ref, d, grad, outs):
    done_ref[...] = jnp.zeros_like(done_ref)
    channels = w_ref.shape[0]
    split = d1_ref.shape[0]
    d[:split, :] = d1_ref[...]
    d[split:, :] = d2_ref[...]
    sent = []
    side = channels // 2
    for k in range(2):
        here = pl.ds(k * side, side)
        grad[here, :] = dot(w_ref[here, :], d[...], ((1,), (0,))).astype(bf16)
        c = pltpu.make_async_copy(grad.at[here, :], grad_hbm.at[here, :], outs.at[k])
        c.start()
        sent.append(c)
    for c in sent:
        c.wait()


def add_kernel(own_ref, keep_ref, right_ref, out_ref):
    ny, nx, nzh, rows, channels = own_ref.shape
    width = right_ref.shape[4] - keep_ref.shape[4]
    cut = channels - width
    core = lax.axis_index("c")
    for y in range(ny):
        for x in range(nx):
            a = jnp.where(core == 0, y, x)
            b = jnp.where(core == 0, x, y)
            for zh in range(nzh):
                here = pl.ds(zh * rows, rows)
                out_ref[a, b, here, :cut] = own_ref[y, x, zh, :, :cut]
                out_ref[a, b, here, cut:channels] = (
                    own_ref[y, x, zh, :, cut:] + right_ref[y, x, zh, :, :width]
                )
                out_ref[a, b, here, channels:] = (
                    keep_ref[y, x, zh] + right_ref[y, x, zh, :, width:]
                )


def deal_kernel(axes, in_ref, *out_refs):
    core = lax.axis_index("c")
    me = jnp.where(core == 0, lax.axis_index(axes[0]), lax.axis_index(axes[1]))
    n = len(out_refs)
    for d in range(n):
        k = lax.rem(me + d, n)
        total = in_ref[0, k]
        for i in range(1, in_ref.shape[0]):
            total = total + in_ref[i, k]
        out_refs[d][...] = total


def partner(me, d):
    low, high = lax.rem(me, 2), me // 2
    low = 1 - low if d % 2 else low
    high = 1 - high if d // 2 else high
    return 2 * high + low


def halve_kernel(done_ref, *refs):
    ins, (keep_ref, send_ref) = refs[:-2], refs[-2:]
    me = lax.axis_index("zh")
    rows = keep_ref.shape[0] // 2
    for i, d in enumerate((0, 3, 1, 2)):
        here = pl.ds(pl.multiple_of(partner(me, d) * rows, rows), rows)
        total = ins[0][here, :]
        for r in ins[1:]:
            total = total + r[here, :]
        (keep_ref, send_ref)[i // 2][(i % 2) * rows : (i % 2 + 1) * rows, :] = total


def quarter_kernel(keep_ref, other_ref, own_ref, send_ref):
    rows = own_ref.shape[0]
    own_ref[...] = keep_ref[:rows, :] + other_ref[:rows, :]
    send_ref[...] = keep_ref[rows:, :] + other_ref[rows:, :]


def spread_kernel(*refs):
    out_ref = refs[-1]
    total = refs[0][...]
    for r in refs[1:-1]:
        total = total + r[...]
    for i in range(out_ref.shape[0]):
        out_ref[i] = total


def finish_kernel(factor, points, in_ref, w1_ref, b1_ref, w2_ref, b2_ref, loss_ref, part):
    ny = in_ref.shape[0] // 2
    rows = in_ref.shape[1]
    share, channels = w1_ref.shape
    variables = w2_ref.shape[1]
    part[...] = jnp.zeros_like(part)
    for y in range(ny):
        here = slice(y * rows, (y + 1) * rows)
        w1_ref[here, :] = (in_ref[y, :, :channels] + in_ref[ny + y, :, :channels]) * factor
        part[here, :] = in_ref[y, :, channels:] + in_ref[ny + y, :, channels:]
    w2_ref[...] = part[:share, :variables] * factor
    turned = jnp.transpose(part[...])
    b1_ref[...] = turned[variables : variables + 1, :share] * factor
    line = turned[variables + 1 : variables + 2, :]
    for g in range(1, lanes // share):
        line = line + pltpu.roll(turned[variables + 1 + g : variables + 2 + g, :], g * share, 1)
    b2_ref[...] = line[:, :variables] * factor
    loss_ref[...] = line[:, variables : variables + 1] * (1.0 / points)


def lines(ny, nx):
    at = lambda y, x, c: (y * nx + x) * 2 + c
    down = [[at(y, x, 0) for y in range(ny)] for x in range(nx)]
    along = [[at(y, x, 1) for x in range(nx)] for y in range(ny)]
    return down + along


def shifts(ny, nx, d):
    at = lambda y, x, c: (y * nx + x) * 2 + c
    pairs = [(at(y, x, 0), at(y, (x + d) % nx, 0)) for y in range(ny) for x in range(nx)]
    return pairs + [(at(y, x, 1), at((y + d) % ny, x, 1)) for y in range(ny) for x in range(nx)]


def on_device(
    hidden, target, area_index, area_table, var_weight, w_first, b_first, w_second, b_second
):
    members = lax.axis_size(ens)
    columns = hidden.shape[2]
    variables = target.shape[0]
    channels = w_first.shape[0]
    slab = columns // members
    nx, nzh, nc, ny = (lax.axis_size(a) for a in ("x", "zh", "c", "y"))
    share = channels // (nx * nzh * nc)
    rows = share // ny
    wide = channels + lanes
    shape = jax.ShapeDtypeStruct
    features = hidden[0]
    grouped = features.reshape(nx * nzh, nc, share, columns)
    w2t = w_second.T
    square = (channels, columns)
    dma = pltpu.SemaphoreType.DMA
    mine = call(
        forward_kernel,
        shape((members, variables, slab), f32),
        [hbm] * 5,
        near,
        scratch=[
            pltpu.VMEM(square, bf16),
            pltpu.VMEM((channels, channels), bf16),
            pltpu.VMEM((1, channels), f32),
            pltpu.VMEM((variables, channels), bf16),
            pltpu.VMEM((1, variables), f32),
            pltpu.VMEM((channels, channels), bf16),
            dma((8,)),
            dma((3,)),
        ],
        flops=2 * channels * channels * columns,
        limit=60,
    )(features, w_first, b_first[None], w2t, b_second[None])
    fields = lax.all_to_all(mine, ens, 0, 0)
    z, g, done = call(
        again_kernel,
        (shape(square, bf16), shape(square, bf16), shape((8, lanes), f32)),
        [pl.BlockSpec(memory_space=pl.ANY)] + [hbm] * 3,
        (hbm, hbm, near),
        scratch=[
            pltpu.VMEM(square, bf16),
            pltpu.VMEM((channels, channels), bf16),
            pltpu.VMEM((1, channels), f32),
            pltpu.VMEM((channels, channels), bf16),
            pltpu.VMEM(square, bf16),
            pltpu.VMEM(square, bf16),
            dma((8,)),
            dma((1,)),
            dma((2, 2)),
        ],
        flops=2 * channels * channels * columns,
        limit=60,
    )(mine, features, w_first, b_first[None])
    dx, misc = call(
        pair_kernel,
        (shape((members, variables, slab), f32), shape((share, lanes), f32)),
        [near] * 2 + [hbm] * 4,
        (near, near),
        scratch=[
            pltpu.VMEM((lanes, lanes), f32),
            pltpu.VMEM((variables, slab), f32),
            pltpu.VMEM((1, columns), jnp.int32),
            pltpu.VMEM(area_table.shape, f32),
            pltpu.VMEM((1, variables), f32),
            dma((4,)),
        ],
        flops=2**34,
    )(done, fields, target, area_index[None], area_table, var_weight[None])
    back = lax.all_to_all(dx, ens, 0, 0)
    part = (ny, nx, nzh, rows)
    cut = channels // 2
    mirror = [(0, 1), (1, 0)]
    d1, dxs, left = call(
        first_kernel,
        (shape((cut, columns), bf16), shape((lanes, columns), bf16), shape(part + (cut,), f32)),
        [near] * 4,
        (near,) * 3,
        flops=channels * channels * columns // 2,
    )(back, w2t, g, grouped)
    left = lax.ppermute(left, "c", mirror)
    d2, right, keep = call(
        second_kernel,
        (
            shape((channels - cut, columns), bf16),
            shape(part + (channels - cut + lanes,), f32),
            shape(part + (lanes,), f32),
        ),
        [near] * 7,
        (near,) * 3,
        scratch=[pltpu.VMEM((nzh, nc, share, lanes), f32)],
        flops=channels * channels * columns // 2,
    )(d1, dxs, w2t, misc, g, z, grouped)
    right = pl.pallas_call(
        after_kernel,
        out_shape=shape(right.shape, f32),
        in_specs=[pl.BlockSpec(memory_space=pl.ANY)] * 2,
        out_specs=pl.BlockSpec(memory_space=pl.ANY),
        input_output_aliases={1: 0},
        compiler_params=pltpu.CompilerParams(vmem_limit_bytes=2**20),
    )(left, right)
    right = lax.ppermute(right, "c", mirror)
    own = call(
        own_kernel,
        shape(part + (channels,), f32),
        [near] * 4,
        near,
    )(d1, d2, grouped, left)
    half = call(
        add_kernel, shape((ny, nx, nzh * rows, wide), f32), [near] * 3, near
    )(own, keep, right)
    half = lax.all_to_all(half, plane, 0, 0, axis_index_groups=lines(ny, nx))
    blocks = call(
        functools.partial(deal_kernel, ("x", "y")),
        (shape((nzh * rows, wide), f32),) * nx,
        [near],
        (near,) * nx,
    )(half)
    grad_feat, built = call(
        grad_kernel,
        (shape(square, bf16), shape((8, lanes), f32)),
        [near] * 4,
        (hbm, near),
        scratch=[pltpu.VMEM(square, bf16), pltpu.VMEM(square, bf16), dma((2,))],
        flops=2 * channels * channels * columns,
    )(blocks[0], d1, d2, w_first)
    blocks = (blocks[0],) + tuple(
        lax.ppermute(blocks[d], plane, shifts(ny, nx, d)) for d in range(1, nx)
    )
    keep, send = call(
        halve_kernel, (shape((2 * rows, wide), f32),) * 2, [near] * (1 + nx), (near,) * 2
    )(built, *blocks)
    send = lax.ppermute(send, "zh", [(i, i ^ 1) for i in range(nzh)])
    keep, send = call(quarter_kernel, (shape((rows, wide), f32),) * 2, [near] * 2, (near,) * 2)(
        keep, send
    )
    blocks = (keep, lax.ppermute(send, "zh", [(i, i ^ 3) for i in range(nzh)]))
    whole = call(spread_kernel, shape((members, rows, wide), f32), [near] * 2, near)(*blocks)
    whole = lax.all_to_all(whole, ens, 0, 0)
    total_points = columns * lax.axis_size(space)
    factor = 1.0 / math.sqrt(members * total_points)
    w1, b1, w2, b2, loss = call(
        functools.partial(finish_kernel, factor, total_points),
        (
            shape((share, channels), f32),
            shape((1, share), f32),
            shape((share, variables), f32),
            shape((1, variables), f32),
            shape((1, 1), f32),
        ),
        [near],
        (near,) * 5,
        scratch=[pltpu.VMEM((lanes, lanes), f32)],
    )(whole)
    return (loss[0, 0], grad_feat[None], w1, b1[0], w2, b2[0])


def solution(mesh):
    fine = Mesh(mesh.devices.reshape(2, 4, 4, 4, 2), ("zl", "y", "x", "zh", "c"))
    in_specs = (P(ens, None, space), P(None, space), P(space), P(), P(), P(), P(), P(), P())
    out_specs = (P(), P(ens, None, space), P(space, None), P(space), P(space, None), P())
    return jax.shard_map(
        on_device, mesh=fine, in_specs=in_specs, out_specs=out_specs, check_vma=False
    )
```

```python
import functools
import math

import jax
import jax.numpy as jnp
from jax import lax
from jax.experimental import pallas as pl
from jax.experimental.pallas import tpu as pltpu
from jax.sharding import Mesh, PartitionSpec as P

smoothing = 0.0025
loss_scale = 64.0
ens = ("zl", "y")
space = ("x", "zh", "c")
plane = ("y", "x", "c")
lanes = 128
tile = 256
f32, bf16 = jnp.float32, jnp.bfloat16
root = math.sqrt(2.0 / math.pi)
cubic = 0.044715


def dot(a, b, contract):
    return lax.dot_general(a, b, (contract, ((), ())), preferred_element_type=f32)


hbm = pl.BlockSpec(memory_space=pltpu.HBM)
near = pl.BlockSpec(memory_space=pltpu.VMEM)


def call(kernel, out_shape, ins, outs, scratch=(), flops=0, limit=24):
    return pl.pallas_call(
        kernel,
        out_shape=out_shape,
        in_specs=ins,
        out_specs=outs,
        scratch_shapes=scratch,
        compiler_params=pltpu.CompilerParams(vmem_limit_bytes=limit * 2**20),
        cost_estimate=pl.CostEstimate(flops=flops, bytes_accessed=2**22, transcendentals=0),
    )


def columns_of(row, width):
    return jnp.transpose(jnp.broadcast_to(row, (width, row.shape[1])))


def arrive(pairs, sems):
    copies = [pltpu.make_async_copy(s, d, sems.at[i]) for i, (s, d) in enumerate(pairs)]
    for c in copies:
        c.start()
    return copies


def turn(w, wt):
    for j in range(0, w.shape[1], tile):
        wt[j : j + tile, :] = jnp.transpose(w[:, j : j + tile])


def arrive_rows(pairs, count, sems):
    cut = []
    for src, dst in pairs:
        step = src.shape[0] // count
        cut += [(src.at[pl.ds(i * step, step)], dst.at[pl.ds(i * step, step)]) for i in range(count)]
    return arrive(cut, sems)


def turn(w, wt):
    for j in range(0, w.shape[1], tile):
        wt[j : j + tile, :] = jnp.transpose(w[:, j : j + tile])


def forward_kernel(f_hbm, w_hbm, b1_hbm, w2_hbm, b2_hbm, x_ref, f, w, b1, w2, b2, wt, big, small):
    copies = arrive_rows([(w_hbm, w), (f_hbm, f)], 4, big)
    copies += arrive([(b1_hbm, b1), (w2_hbm, w2), (b2_hbm, b2)], small)
    for c in copies:
        c.wait()
    turn(w, wt)
    shift = columns_of(b1[...], lanes)
    bias = columns_of(b2[...], lanes)
    pre = dot(wt[...], f[...], ((1,), (0,))) + jnp.tile(shift, (1, f.shape[1] // lanes))
    t = jnp.tanh(pre * (root + (root * cubic) * (pre * pre)))
    z = (0.5 * pre * (1.0 + t)).astype(bf16)
    x = dot(w2[...], z, ((1,), (0,)))
    for m in range(x_ref.shape[0]):
        x_ref[m] = x[:, m * lanes : (m + 1) * lanes] + bias


def again_kernel(x_hbm, f_hbm, w_hbm, b1_hbm, z_hbm, g_hbm, done_ref, f, w, b1, wt, z, g, big, small, outs):
    copies = arrive_rows([(w_hbm, w), (f_hbm, f)], 4, big) + arrive([(b1_hbm, b1)], small)
    for c in copies:
        c.wait()
    done_ref[...] = jnp.zeros_like(done_ref)
    turn(w, wt)
    half = f.shape[1] // 2
    shift = jnp.tile(columns_of(b1[...], lanes), (1, half // lanes))
    sent = []
    for k in range(2):
        here = pl.ds(k * half, half)
        pre = dot(wt[...], f[:, here], ((1,), (0,))) + shift
        square = pre * pre
        rise = 0.5 + 0.5 * jnp.tanh(pre * (root + (root * cubic) * square))
        z[:, here] = (pre * rise).astype(bf16)
        inner = 2.0 * root + (6.0 * root * cubic) * square
        g[:, here] = (rise + (pre * inner) * (rise * (1.0 - rise))).astype(bf16)
        for i, (src, dst) in enumerate(((z, z_hbm), (g, g_hbm))):
            c = pltpu.make_async_copy(src.at[:, here], dst.at[:, here], outs.at[k, i])
            c.start()
            sent.append(c)
    for c in sent:
        c.wait()


def pair_kernel(
    done_ref, x_ref, goal_hbm, index_hbm, table_hbm, weight_hbm, dx_ref, misc_ref,
    col, goal_ref, index_ref, table_ref, weight_ref, sems,
):
    members, variables, slab = x_ref.shape
    me = lax.axis_index(ens)
    here = pl.ds(pl.multiple_of(me * slab, slab), slab)
    rows = table_ref.shape[0]
    copies = arrive(
        [
            (index_hbm, index_ref),
            (table_hbm, table_ref),
            (weight_hbm, weight_ref),
            (goal_hbm.at[:, here], goal_ref),
        ],
        sems,
    )
    fields = [x_ref[m] for m in range(members)]
    pull = [None] * members
    spread = None
    for a in range(members):
        for b in range(a + 1, members):
            d = fields[a] - fields[b]
            square = d * d + smoothing
            inverse = lax.rsqrt(square)
            spread = square * inverse if spread is None else spread + square * inverse
            term = d * inverse
            pull[a] = term if pull[a] is None else pull[a] + term
            pull[b] = -term if pull[b] is None else pull[b] - term
    spread = 2.0 * spread + members * math.sqrt(smoothing)
    for c in copies:
        c.wait()
    hot = lax.broadcasted_iota(jnp.int32, (rows, slab), 0) == index_ref[:, here]
    area = lax.dot_general(
        table_ref[...].reshape(1, rows),
        hot.astype(f32),
        (((1,), (0,)), ((), ())),
        precision=lax.Precision.HIGHEST,
        preferred_element_type=f32,
    )
    coef = columns_of(weight_ref[...], slab) * area
    goal = goal_ref[...]
    pairs = members * (members - 1)
    skills = None
    total = None
    for m in range(members):
        miss = fields[m] - goal
        square = miss * miss + smoothing
        inverse = lax.rsqrt(square)
        skills = square * inverse if skills is None else skills + square * inverse
        slope = miss * inverse * (1.0 / members) - pull[m] * (1.0 / pairs)
        grad = (loss_scale * coef * slope).astype(bf16).astype(f32)
        dx_ref[m] = grad
        total = grad if total is None else total + grad
    crps = coef * (skills * (1.0 / members) - spread * (0.5 / pairs))
    col[...] = jnp.zeros_like(col)
    col[:variables, :] = jnp.broadcast_to(jnp.sum(total, axis=1, keepdims=True), (variables, lanes))
    loss = jnp.sum(jnp.sum(crps, axis=0, keepdims=True), axis=1, keepdims=True)
    col[variables : variables + 1, :] = jnp.broadcast_to(loss, (1, lanes))
    share = misc_ref.shape[0]
    lane = lax.broadcasted_iota(jnp.int32, (share, lanes), 1)
    out = jnp.zeros((share, lanes), f32)
    for g in range(lanes // share):
        out = jnp.where(lane == variables + 1 + g, col[g * share : (g + 1) * share, :], out)
    misc_ref[...] = out


def scatter_rows(first, put, nx, nzh, ny, rows):
    for y in range(ny):
        for zh in range(nzh):
            for x in range(nx):
                r = ((x * nzh + zh) * ny + y) * rows
                put(y, x, zh, first[r : r + rows])


def gradient_rows(w2_ref, g_ref, dx, here):
    dz = dot(jnp.transpose(w2_ref[:, here]), dx, ((1,), (0,)))
    return (dz * g_ref[here, :].astype(f32)).astype(bf16)


def first_kernel(back_ref, w2_ref, g_ref, f_ref, d_ref, dx_ref, send_ref):
    members, variables, slab = back_ref.shape
    ny, nx, nzh, rows, wide = send_ref.shape
    core = lax.axis_index("c")
    dx_ref[...] = jnp.zeros_like(dx_ref)
    for m in range(members):
        dx_ref[:variables, m * slab : (m + 1) * slab] = back_ref[m].astype(bf16)
    half = f_ref[:, 1 - core].reshape(nx * nzh * ny * rows, dx_ref.shape[1])
    for j in range(wide // tile):
        here = slice(j * tile, (j + 1) * tile)
        d = gradient_rows(w2_ref, g_ref, dx_ref[:variables, :], here)
        d_ref[here, :] = d
        first = dot(half, d, ((1,), (1,)))

        def put(y, x, zh, value):
            send_ref[y, x, zh, :, here] = value

        scatter_rows(first, put, nx, nzh, ny, rows)


def second_kernel(
    d1_ref, dx_ref, w2_ref, misc_ref, g_ref, z_ref, f_ref, d_ref, send_ref, keep_ref, piece
):
    ny, nx, nzh, rows, wide = send_ref.shape
    wide = wide - lanes
    variables = w2_ref.shape[0]
    channels, points = z_ref.shape
    share = ny * rows
    core = lax.axis_index("c")
    half = f_ref[:, 1 - core].reshape(nx * nzh * share, points)
    base = channels - wide
    for j in range(wide // tile):
        here = slice(j * tile, (j + 1) * tile)
        there = slice(base + j * tile, base + (j + 1) * tile)
        d = gradient_rows(w2_ref, g_ref, dx_ref[:variables, :], there)
        d_ref[here, :] = d
        first = dot(half, d, ((1,), (1,)))

        def put(y, x, zh, value):
            send_ref[y, x, zh, :, here] = value

        scatter_rows(first, put, nx, nzh, ny, rows)
    lane = lax.broadcasted_iota(jnp.int32, (tile, lanes), 1)
    extra = jnp.tile(misc_ref[...], (tile // share, 1))
    for j in range(channels // tile):
        here = slice(j * tile, (j + 1) * tile)
        d = d1_ref[here, :] if j * tile < base else d_ref[j * tile - base : (j + 1) * tile - base, :]
        sums = jnp.sum(d.astype(f32), axis=1, keepdims=True)
        second = dot(z_ref[here, :], dx_ref[...], ((1,), (1,)))
        second = jnp.where(lane == variables, sums, second + extra)
        piece[...] = second.reshape(nzh, 2, share, lanes)
        go, stay = piece[:, 1 - core], piece[:, core]
        for y in range(ny):
            for zh in range(nzh):
                send_ref[y, j, zh, :, wide:] = go[zh, y * rows : (y + 1) * rows]
                keep_ref[y, j, zh] = stay[zh, y * rows : (y + 1) * rows]


def after_kernel(left_ref, right_ref, out_ref):
    pass


def own_kernel(d1_ref, d2_ref, f_ref, left_ref, own_ref):
    ny, nx, nzh, rows, channels = own_ref.shape
    core = lax.axis_index("c")
    cut, points = d1_ref.shape
    half = f_ref[:, core].reshape(nx * nzh * ny * rows, points)
    for j in range(channels // tile):
        here = slice(j * tile, (j + 1) * tile)
        early = j * tile < cut
        d = d1_ref[here, :] if early else d2_ref[j * tile - cut : (j + 1) * tile - cut, :]
        first = dot(half, d, ((1,), (1,)))

        def put(y, x, zh, value):
            own_ref[y, x, zh, :, here] = value + left_ref[y, x, zh, :, here] if early else value

        scatter_rows(first, put, nx, nzh, ny, rows)


def grad_kernel(late_ref, d1_ref, d2_ref, w_ref, grad_hbm, done_ref, d, grad, outs):
    done_ref[...] = jnp.zeros_like(done_ref)
    channels = w_ref.shape[0]
    split = d1_ref.shape[0]
    d[:split, :] = d1_ref[...]
    d[split:, :] = d2_ref[...]
    sent = []
    side = channels // 2
    for k in range(2):
        here = pl.ds(k * side, side)
        grad[here, :] = dot(w_ref[here, :], d[...], ((1,), (0,))).astype(bf16)
        c = pltpu.make_async_copy(grad.at[here, :], grad_hbm.at[here, :], outs.at[k])
        c.start()
        sent.append(c)
    for c in sent:
        c.wait()


def partner(me, d):
    low, high = lax.rem(me, 2), me // 2
    low = 1 - low if d % 2 else low
    high = 1 - high if d // 2 else high
    return 2 * high + low


def add_kernel(own_ref, keep_ref, right_ref, *out_refs):
    ny, nx, nzh, rows, channels = own_ref.shape
    width = right_ref.shape[4] - keep_ref.shape[4]
    cut = channels - width
    first = lax.axis_index("c") == 0
    me = jnp.where(first, lax.axis_index("y"), lax.axis_index("x"))
    for d in range(ny):
        block = partner(me, d)
        for b in range(nx):
            y, x = jnp.where(first, block, b), jnp.where(first, b, block)
            for zh in range(nzh):
                here = pl.ds(zh * rows, rows)
                out_refs[d][b, here, :cut] = own_ref[y, x, zh, :, :cut]
                out_refs[d][b, here, cut:channels] = (
                    own_ref[y, x, zh, :, cut:] + right_ref[y, x, zh, :, :width]
                )
                out_refs[d][b, here, channels:] = (
                    keep_ref[y, x, zh] + right_ref[y, x, zh, :, width:]
                )


def deal_kernel(axes, done_ref, *refs):
    n = len(refs) // 2
    core = lax.axis_index("c")
    me = jnp.where(core == 0, lax.axis_index(axes[0]), lax.axis_index(axes[1]))
    for d in range(n):
        k = lax.rem(me + d, n)
        total = refs[0][k]
        for i in range(1, n):
            total = total + refs[i][k]
        refs[n + d][...] = total


def redeal_kernel(axis, *refs):
    n = len(refs) // 2
    me = lax.axis_index(axis)
    rows = refs[n].shape[0]
    for d in range(n):
        here = pl.ds(pl.multiple_of(lax.rem(me + d, n) * rows, rows), rows)
        total = refs[0][here, :]
        for i in range(1, n):
            total = total + refs[i][here, :]
        refs[n + d][...] = total


def spread_kernel(*refs):
    out_ref = refs[-1]
    total = refs[0][...]
    for r in refs[1:-1]:
        total = total + r[...]
    for i in range(out_ref.shape[0]):
        out_ref[i] = total


def finish_kernel(factor, points, in_ref, w1_ref, b1_ref, w2_ref, b2_ref, loss_ref, part):
    ny = in_ref.shape[0] // 2
    rows = in_ref.shape[1]
    share, channels = w1_ref.shape
    variables = w2_ref.shape[1]
    part[...] = jnp.zeros_like(part)
    for y in range(ny):
        here = slice(y * rows, (y + 1) * rows)
        w1_ref[here, :] = (in_ref[y, :, :channels] + in_ref[ny + y, :, :channels]) * factor
        part[here, :] = in_ref[y, :, channels:] + in_ref[ny + y, :, channels:]
    w2_ref[...] = part[:share, :variables] * factor
    turned = jnp.transpose(part[...])
    b1_ref[...] = turned[variables : variables + 1, :share] * factor
    line = turned[variables + 1 : variables + 2, :]
    for g in range(1, lanes // share):
        line = line + pltpu.roll(turned[variables + 1 + g : variables + 2 + g, :], g * share, 1)
    b2_ref[...] = line[:, :variables] * factor
    loss_ref[...] = line[:, variables : variables + 1] * (1.0 / points)


def swaps(ny, nx, d):
    at = lambda y, x, c: (y * nx + x) * 2 + c
    pairs = [(at(y, x, 0), at(y ^ d, x, 0)) for y in range(ny) for x in range(nx)]
    return pairs + [(at(y, x, 1), at(y, x ^ d, 1)) for y in range(ny) for x in range(nx)]


def shifts(ny, nx, d):
    at = lambda y, x, c: (y * nx + x) * 2 + c
    pairs = [(at(y, x, 0), at(y, (x + d) % nx, 0)) for y in range(ny) for x in range(nx)]
    return pairs + [(at(y, x, 1), at((y + d) % ny, x, 1)) for y in range(ny) for x in range(nx)]


def on_device(
    hidden, target, area_index, area_table, var_weight, w_first, b_first, w_second, b_second
):
    members = lax.axis_size(ens)
    columns = hidden.shape[2]
    variables = target.shape[0]
    channels = w_first.shape[0]
    slab = columns // members
    nx, nzh, nc, ny = (lax.axis_size(a) for a in ("x", "zh", "c", "y"))
    share = channels // (nx * nzh * nc)
    rows = share // ny
    wide = channels + lanes
    shape = jax.ShapeDtypeStruct
    features = hidden[0]
    grouped = features.reshape(nx * nzh, nc, share, columns)
    w2t = w_second.T
    square = (channels, columns)
    dma = pltpu.SemaphoreType.DMA
    mine = call(
        forward_kernel,
        shape((members, variables, slab), f32),
        [hbm] * 5,
        near,
        scratch=[
            pltpu.VMEM(square, bf16),
            pltpu.VMEM((channels, channels), bf16),
            pltpu.VMEM((1, channels), f32),
            pltpu.VMEM((variables, channels), bf16),
            pltpu.VMEM((1, variables), f32),
            pltpu.VMEM((channels, channels), bf16),
            dma((8,)),
            dma((3,)),
        ],
        flops=2 * channels * channels * columns,
        limit=60,
    )(features, w_first, b_first[None], w2t, b_second[None])
    fields = lax.all_to_all(mine, ens, 0, 0)
    z, g, done = call(
        again_kernel,
        (shape(square, bf16), shape(square, bf16), shape((8, lanes), f32)),
        [pl.BlockSpec(memory_space=pl.ANY)] + [hbm] * 3,
        (hbm, hbm, near),
        scratch=[
            pltpu.VMEM(square, bf16),
            pltpu.VMEM((channels, channels), bf16),
            pltpu.VMEM((1, channels), f32),
            pltpu.VMEM((channels, channels), bf16),
            pltpu.VMEM(square, bf16),
            pltpu.VMEM(square, bf16),
            dma((8,)),
            dma((1,)),
            dma((2, 2)),
        ],
        flops=2 * channels * channels * columns,
        limit=60,
    )(mine, features, w_first, b_first[None])
    dx, misc = call(
        pair_kernel,
        (shape((members, variables, slab), f32), shape((share, lanes), f32)),
        [near] * 2 + [hbm] * 4,
        (near, near),
        scratch=[
            pltpu.VMEM((lanes, lanes), f32),
            pltpu.VMEM((variables, slab), f32),
            pltpu.VMEM((1, columns), jnp.int32),
            pltpu.VMEM(area_table.shape, f32),
            pltpu.VMEM((1, variables), f32),
            dma((4,)),
        ],
        flops=2**34,
    )(done, fields, target, area_index[None], area_table, var_weight[None])
    back = lax.all_to_all(dx, ens, 0, 0)
    part = (ny, nx, nzh, rows)
    cut = channels // 2
    mirror = [(0, 1), (1, 0)]
    d1, dxs, left = call(
        first_kernel,
        (shape((cut, columns), bf16), shape((lanes, columns), bf16), shape(part + (cut,), f32)),
        [near] * 4,
        (near,) * 3,
        flops=channels * channels * columns // 2,
    )(back, w2t, g, grouped)
    left = lax.ppermute(left, "c", mirror)
    d2, right, keep = call(
        second_kernel,
        (
            shape((channels - cut, columns), bf16),
            shape(part + (channels - cut + lanes,), f32),
            shape(part + (lanes,), f32),
        ),
        [near] * 7,
        (near,) * 3,
        scratch=[pltpu.VMEM((nzh, nc, share, lanes), f32)],
        flops=channels * channels * columns // 2,
    )(d1, dxs, w2t, misc, g, z, grouped)
    right = pl.pallas_call(
        after_kernel,
        out_shape=shape(right.shape, f32),
        in_specs=[pl.BlockSpec(memory_space=pl.ANY)] * 2,
        out_specs=pl.BlockSpec(memory_space=pl.ANY),
        input_output_aliases={1: 0},
        compiler_params=pltpu.CompilerParams(vmem_limit_bytes=2**20),
    )(left, right)
    right = lax.ppermute(right, "c", mirror)
    own = call(
        own_kernel,
        shape(part + (channels,), f32),
        [near] * 4,
        near,
    )(d1, d2, grouped, left)
    blocks = call(
        add_kernel, (shape((nx, nzh * rows, wide), f32),) * ny, [near] * 3, (near,) * ny
    )(own, keep, right)
    grad_feat, built = call(
        grad_kernel,
        (shape(square, bf16), shape((8, lanes), f32)),
        [near] * 4,
        (hbm, near),
        scratch=[pltpu.VMEM(square, bf16), pltpu.VMEM(square, bf16), dma((2,))],
        flops=2 * channels * channels * columns,
    )(blocks[0], d1, d2, w_first)
    moved = {d: lax.ppermute(blocks[d], plane, swaps(ny, nx, d)) for d in (1, 3, 2)}
    blocks = (blocks[0],) + tuple(moved[d] for d in range(1, ny))
    blocks = call(
        functools.partial(deal_kernel, ("x", "y")),
        (shape((nzh * rows, wide), f32),) * nx,
        [near] * (1 + ny),
        (near,) * nx,
    )(built, *blocks)
    blocks = (blocks[0],) + tuple(
        lax.ppermute(blocks[d], plane, shifts(ny, nx, d)) for d in range(1, nx)
    )
    blocks = call(
        functools.partial(redeal_kernel, "zh"),
        (shape((rows, wide), f32),) * nzh,
        [near] * nx,
        (near,) * nzh,
    )(*blocks)
    blocks = (blocks[0],) + tuple(
        lax.ppermute(blocks[d], "zh", [(i, (i + d) % nzh) for i in range(nzh)])
        for d in range(1, nzh)
    )
    whole = call(spread_kernel, shape((members, rows, wide), f32), [near] * nzh, near)(*blocks)
    whole = lax.all_to_all(whole, ens, 0, 0)
    total_points = columns * lax.axis_size(space)
    factor = 1.0 / math.sqrt(members * total_points)
    w1, b1, w2, b2, loss = call(
        functools.partial(finish_kernel, factor, total_points),
        (
            shape((share, channels), f32),
            shape((1, share), f32),
            shape((share, variables), f32),
            shape((1, variables), f32),
            shape((1, 1), f32),
        ),
        [near],
        (near,) * 5,
        scratch=[pltpu.VMEM((lanes, lanes), f32)],
    )(whole)
    return (loss[0, 0], grad_feat[None], w1, b1[0], w2, b2[0])


def solution(mesh):
    fine = Mesh(mesh.devices.reshape(2, 4, 4, 4, 2), ("zl", "y", "x", "zh", "c"))
    in_specs = (P(ens, None, space), P(None, space), P(space), P(), P(), P(), P(), P(), P())
    out_specs = (P(), P(ens, None, space), P(space, None), P(space), P(space, None), P())
    return jax.shard_map(
        on_device, mesh=fine, in_specs=in_specs, out_specs=out_specs, check_vma=False
    )
```
